256 devices in a mesh: ctx: 32 (over x, z_lo, core), tp: 8 (over z_hi, y).
Axes of the slice: x: 4, y: 4, z: 8 (z_hi: 2, z_lo: 4; z = z_hi * 4 + z_lo), core: 2. Of those that a mesh axis runs over, the one named last changes fastest.
Arguments:
- q_nope: bfloat16 [4096, 128, 128], P('ctx', 'tp'), may hold values from -6 to 6
- q_rope: bfloat16 [4096, 8192], P('ctx', 'tp'), may hold values from -8 to 8
- latent: bfloat16 [4096, 512], P('ctx'), may hold values from -6 to 6
- k_rope: bfloat16 [4096, 64], P('ctx'), may hold values from -8 to 8
- out_grad: bfloat16 [4096, 128, 128], P('ctx', 'tp'), may hold values from -6 to 6
- w_key: bfloat16 [128, 128, 512], P('tp'), may hold values from -0.25 to 0.25
- w_value: bfloat16 [128, 512, 128], P('tp'), may hold values from -0.25 to 0.25
- lengths: int32 [6], replicated, may hold values from 1 to 768, 4096 in all
Outputs:
- grad_q_nope: bfloat16 [4096, 128, 128], P('ctx', 'tp')
- grad_q_rope: bfloat16 [4096, 8192], P('ctx', 'tp')
- grad_latent: bfloat16 [4096, 512], P('ctx')
- grad_k_rope: bfloat16 [4096, 64], P('ctx')
- grad_w_key: bfloat16 [128, 128, 512], P('tp', 'ctx')
- grad_w_value: bfloat16 [128, 512, 128], P('tp', 'ctx')
The draws below stay inside these ranges and needn't reach their ends.
Inputs may be any that keep to these rules, and one draw needn't show every extreme that they name: `lengths`: every document has 1 to 768 tokens, one exactly 768, and they sum to 4096.
All inputs are finite; a program needn't handle non-finite values.
Results may differ from the reference program's by a relative error of at most 0.034.
Values may be sent and summed in bfloat16 or wider, within the bound.
A program may use at most 192 MiB of HBM per device.

```python
import math
import jax
import jax.numpy as jnp
import numpy as np
from jax import lax

HEADS = 128
NOPE = 128
ROPE = 64
LATENT = 512
TOK_DEV = 128
SPAN = 6
COUNT = 6
TOKENS = 4096
MOST = 768
N_CTX = 32


def draw_q_rope(key, part):
    noise_key = jax.random.fold_in(key, 1)
    values = jnp.clip(jax.random.normal(noise_key, (TOKENS, HEADS * ROPE), jnp.float32), -6.0, 6.0)
    return values.astype(jnp.bfloat16)


def draw_k_rope(key, part):
    noise_key = jax.random.fold_in(key, 2)
    values = jnp.clip(jax.random.normal(noise_key, (TOKENS, ROPE), jnp.float32), -6.0, 6.0)
    return values.astype(jnp.bfloat16)


def shard_levels(rng, extent, cuts, smallest, top_value):
    loudness, own = 1.0, jax.random.fold_in(rng, 6)
    for axis_at, blocks in cuts:
        draws = jnp.exp(jax.random.uniform(jax.random.fold_in(own, axis_at), (blocks,), jnp.float32, smallest / len(cuts), top_value / len(cuts)))
        loudness = loudness * jnp.repeat(draws, extent[axis_at] // blocks).reshape([-1 if axis == axis_at else 1 for axis in range(len(extent))])
    return loudness


def length_profile(amount, total, reach, skew):
    portions = [(1 << 20) // math.isqrt(grade ** skew) + 1 for grade in range(2, amount + 1)]
    rest, given = total - reach - (amount - 1), [1] * (amount - 1)
    while rest > 0:
        movable = [i for i in range(amount - 1) if given[i] < reach]
        whole, left = sum([portions[i] for i in movable]), rest
        for i in movable:
            extra = min(reach - given[i], max(1, left * portions[i] // whole), rest)
            given[i] = given[i] + extra
            rest = rest - extra
    return np.array([reach] + given)


def ragged_sizes(key, amount, total, most, slope):
    if amount == 2:
        one = jax.random.randint(key, (), max(1, total - most), min(most, total - 1) + 1)
        return jnp.stack([one, total - one])
    sizes = jnp.asarray(length_profile(amount, total, most, slope), jnp.int32)
    pairs = (amount - 1) // 2
    giver, taker = sizes[1:1 + 2 * pairs:2], sizes[2:2 + 2 * pairs:2]
    room = jnp.minimum(giver - 1, most - taker)
    shifted = jax.random.randint(jax.random.fold_in(key, 1), (pairs,), 0, 1 << 20) % (room + 1)
    sizes = sizes.at[1:1 + 2 * pairs:2].set(giver - shifted).at[2:2 + 2 * pairs:2].set(taker + shifted)
    return sizes[jax.random.permutation(jax.random.fold_in(key, 2), amount)]


def scatter_about(rng, dims, deviation, reach, cuts=(), kind=jnp.bfloat16):
    result = deviation * jax.random.normal(rng, dims, jnp.float32)
    if cuts:
        result = result * shard_levels(rng, dims, cuts, -0.22, 0.18)
    return jnp.clip(result, -reach, reach).astype(kind)


def setup_inputs(seed: int = 0) -> dict:
    splits = jax.random.split(jax.random.key(seed), 9)
    return {
        "q_nope": scatter_about(splits[0], (TOKENS, HEADS, NOPE), 1.0, 6.0, ((0, 32), (1, 8))),
        "q_rope": draw_q_rope(jax.random.fold_in(splits[8], 71), 0),
        "latent": scatter_about(splits[2], (TOKENS, LATENT), 1.0, 6.0, ((0, 32),)),
        "k_rope": draw_k_rope(jax.random.fold_in(splits[8], 71), 0),
        "out_grad": scatter_about(splits[4], (TOKENS, HEADS, NOPE), 1.0, 6.0, ((0, 32), (1, 8))),
        "w_key": scatter_about(splits[5], (HEADS, NOPE, LATENT), LATENT ** -0.5, 0.25, ((0, 8),)),
        "w_value": scatter_about(splits[6], (HEADS, LATENT, NOPE), LATENT ** -0.5, 0.25, ((0, 8),)),
        "lengths": ragged_sizes(splits[7], COUNT, TOKENS, MOST, 2).astype(jnp.int32),
    }


def doc_starts(lengths, positions):
    ends = jnp.cumsum(lengths).astype(jnp.int32)
    begins = (ends - lengths).astype(jnp.int32)
    inside = (begins[None, :] <= positions[:, None]) & (positions[:, None] < ends[None, :])
    return jnp.sum(jnp.where(inside, begins[None, :], 0), axis=1).astype(jnp.int32)


def reference(q_nope, q_rope, latent, k_rope, out_grad, w_key, w_value, lengths):
    softmax_scale = float(NOPE + ROPE) ** -0.5
    margin = SPAN * TOK_DEV
    window = (SPAN + 1) * TOK_DEV
    lat_pad = jnp.concatenate([jnp.zeros((margin, LATENT), latent.dtype), latent], 0)
    rope_pad = jnp.concatenate([jnp.zeros((margin, ROPE), k_rope.dtype), k_rope], 0)
    key_weight = w_key.astype(jnp.float32)
    value_weight = w_value.astype(jnp.float32)

    def block(carry, index):
        lat_acc, rope_acc, wkey_acc, wvalue_acc = carry
        first = (index * TOK_DEV).astype(jnp.int32)
        query_nope = lax.dynamic_slice_in_dim(q_nope, first, TOK_DEV, 0).astype(jnp.float32)
        query_rope = lax.dynamic_slice_in_dim(q_rope, first, TOK_DEV, 0).reshape(TOK_DEV, HEADS, ROPE).astype(jnp.float32)
        cotangent = lax.dynamic_slice_in_dim(out_grad, first, TOK_DEV, 0).astype(jnp.float32)
        key_lat = lax.dynamic_slice_in_dim(lat_pad, first, window, 0).astype(jnp.float32)
        key_rope = lax.dynamic_slice_in_dim(rope_pad, first, window, 0).astype(jnp.float32)
        query_pos = first + jnp.arange(TOK_DEV, dtype=jnp.int32)
        key_pos = first - margin + jnp.arange(window, dtype=jnp.int32)
        doc_start = doc_starts(lengths, query_pos)
        allowed = (key_pos[None, :] >= doc_start[:, None]) & (key_pos[None, :] <= query_pos[:, None])
        lat_query = jnp.einsum('thn,hnl->thl', query_nope, key_weight).astype(jnp.bfloat16)
        raw = softmax_scale * (jnp.einsum('thl,kl->htk', lat_query.astype(jnp.float32), key_lat)
                               + jnp.einsum('thr,kr->htk', query_rope, key_rope))
        scores = jnp.where(allowed[None], raw, -jnp.inf)
        row_max = jnp.max(scores, axis=-1)
        log_total = row_max + jnp.log(jnp.sum(jnp.exp(scores - row_max[..., None]), axis=-1))
        prob = jnp.exp(scores - log_total[..., None])
        prob16 = prob.astype(jnp.bfloat16)
        out_lat = jnp.einsum('htk,kl->thl', prob16.astype(jnp.float32), key_lat).astype(jnp.bfloat16)
        grad_lat_out = jnp.einsum('thn,hln->thl', cotangent, value_weight).astype(jnp.bfloat16)
        wvalue_acc = wvalue_acc + jnp.einsum('thl,thn->hln', out_lat.astype(jnp.float32), cotangent)
        correction = jnp.sum(out_lat.astype(jnp.float32) * grad_lat_out.astype(jnp.float32), axis=-1).T
        grad_prob = jnp.einsum('thl,kl->htk', grad_lat_out.astype(jnp.float32), key_lat)
        grad_scores = (softmax_scale * prob * (grad_prob - correction[..., None])).astype(jnp.bfloat16)
        grad_float = grad_scores.astype(jnp.float32)
        grad_lat_query = jnp.einsum('htk,kl->thl', grad_float, key_lat).astype(jnp.bfloat16)
        grad_query_rope = jnp.einsum('htk,kr->thr', grad_float, key_rope).astype(jnp.bfloat16)
        grad_query_nope = jnp.einsum('thl,hnl->thn', grad_lat_query.astype(jnp.float32), key_weight).astype(jnp.bfloat16)
        wkey_acc = wkey_acc + jnp.einsum('thn,thl->hnl', query_nope, grad_lat_query.astype(jnp.float32))
        grad_keys = (jnp.einsum('htk,thl->kl', grad_float, lat_query.astype(jnp.float32))
                     + jnp.einsum('htk,thl->kl', prob16.astype(jnp.float32), grad_lat_out.astype(jnp.float32)))
        grad_rope = jnp.einsum('htk,thr->kr', grad_float, query_rope)
        lat_acc = lax.dynamic_update_slice_in_dim(
            lat_acc, lax.dynamic_slice_in_dim(lat_acc, first, window, 0) + grad_keys, first, 0)
        rope_acc = lax.dynamic_update_slice_in_dim(
            rope_acc, lax.dynamic_slice_in_dim(rope_acc, first, window, 0) + grad_rope, first, 0)
        return (lat_acc, rope_acc, wkey_acc, wvalue_acc), (grad_query_nope, grad_query_rope.reshape(TOK_DEV, HEADS * ROPE))

    start_carry = (jnp.zeros((TOKENS + margin, LATENT), jnp.float32),
                   jnp.zeros((TOKENS + margin, ROPE), jnp.float32),
                   jnp.zeros((HEADS, NOPE, LATENT), jnp.float32),
                   jnp.zeros((HEADS, LATENT, NOPE), jnp.float32))
    carry, outputs = lax.scan(block, start_carry, jnp.arange(N_CTX, dtype=jnp.int32))
    lat_acc, rope_acc, wkey_acc, wvalue_acc = carry
    grad_q_nope = outputs[0].reshape(TOKENS, HEADS, NOPE)
    grad_q_rope = outputs[1].reshape(TOKENS, HEADS * ROPE)
    return (grad_q_nope, grad_q_rope,
            lat_acc[margin:].astype(jnp.bfloat16), rope_acc[margin:].astype(jnp.bfloat16),
            wkey_acc.astype(jnp.bfloat16), wvalue_acc.astype(jnp.bfloat16))
```

```python
import jax
import jax.numpy as jnp
from jax import lax
from jax.experimental import pallas as pl
from jax.experimental.pallas import tpu as pltpu
from jax.sharding import PartitionSpec as P

NOPE = 128
ROPE = 64
LATENT = 512
WIDE = LATENT + 2 * ROPE
TOK = 128
SPAN = 6
WINDOW = (SPAN + 1) * TOK
HEADS = 16
PACK = 4
GROUPS = HEADS // PACK
COLS = PACK * TOK
SCALE = float(NOPE + ROPE) ** -0.5
MESH = pl.DeviceIdType.MESH
F32 = jnp.float32
BF16 = jnp.bfloat16


def nn(a, b):
    return lax.dot_general(a, b, (((1,), (0,)), ((), ())), preferred_element_type=F32)


def nt(a, b):
    return lax.dot_general(a, b, (((1,), (1,)), ((), ())), preferred_element_type=F32)


def add(*terms):
    total = terms[0].astype(F32)
    for term in terms[1:]:
        total = total + term.astype(F32)
    return total


def iota(shape, dim):
    return lax.broadcasted_iota(jnp.int32, shape, dim)


def kernel(
    lengths,
    q,
    q_rope,
    latent,
    k_rope,
    og,
    wk,
    wv,
    gq,
    gq_rope,
    g_latent,
    g_rope,
    g_wk,
    g_wv,
    kall,
    kw,
    kwt,
    q_all,
    gt_all,
    p_all,
    ds_all,
    s_buf,
    gp_buf,
    bias,
    dk,
    w_out,
    w_r0,
    w_r1,
    w_r2,
    w_v,
    w_rz,
    kg,
    k_r0,
    k_r1,
    k_r2,
    k_sum,
    k_r3,
    k_mid,
    k_r4,
    k_fin,
    k_out,
    own_s,
    own_r,
    ctx_s,
    ctx_r,
    yag_s,
    yag_r,
    sib_s,
    sib_r,
    w0_s,
    w0_r,
    w1_s,
    w1_r,
    w2_s,
    w2_r,
    wz_s,
    wz_r,
    e0_s,
    e0_r,
    e1_s,
    e1_r,
    e2_s,
    e2_r,
    e3_s,
    e3_r,
    e4_s,
    e4_r,
    e5_s,
    e5_r,
):
    me = lax.axis_index("ctx")
    tp = lax.axis_index("tp")
    core = lax.rem(me, 2)
    chip = lax.div(me, 2)
    z = lax.rem(chip, 4)
    x = lax.div(chip, 4)
    y = lax.rem(tp, 4)
    zh = lax.div(tp, 4)
    other = 1 - core

    def place(x_=x, z_=z, core_=core, y_=y, zh_=zh):
        return ((x_ * 4 + z_) * 2 + core_, zh_ * 4 + y_)

    def up(value, step):
        return lax.rem(value + step, 4)

    def chip_at(step):
        return (lax.rem(chip + step + 16, 16) * 2 + core, tp)

    sibling = place(core_=other)
    x_next, x_prev, x_far = up(x, 1), up(x, 3), up(x, 2)
    y_next, y_prev, y_far = up(y, 1), up(y, 3), up(y, 2)

    barrier = pltpu.get_barrier_semaphore()
    peers = [sibling, place(x_=x_next), place(x_=x_prev), place(zh_=1 - zh)]
    for step in (1, 2, 3):
        peers += [place(z_=up(z, step)), chip_at(step), chip_at(-step)]
        peers += [place(y_=up(y, step)), place(y_=up(y, step), core_=other)]
    for peer in peers:
        pl.semaphore_signal(barrier, inc=1, device_id=peer, device_id_type=MESH)

    def remote(src, dst, send, recv, peer):
        return pltpu.make_async_remote_copy(
            src_ref=src,
            dst_ref=dst,
            send_sem=send,
            recv_sem=recv,
            device_id=peer,
            device_id_type=MESH,
        )

    for quarter in range(4):
        rows = slice(quarter * 32, quarter * 32 + 32)
        kall[3, core, quarter, :, :LATENT] = latent[rows, :]
        kall[3, core, quarter, :, LATENT:] = jnp.concatenate([k_rope[rows, :]] * 2, axis=1)
    pl.semaphore_wait(barrier, len(peers))

    own = remote(kall.at[3, core], kall.at[3, core], own_s, own_r, sibling)
    ahead = [
        remote(
            kall.at[3, core, y],
            kall.at[3 - step, core, y],
            ctx_s.at[step - 1],
            ctx_r.at[step - 1],
            chip_at(step),
        )
        for step in (1, 2, 3)
    ]
    for copy in ahead:
        copy.start()
    own.start()

    lane = iota((TOK, 2 * ROPE), 1)

    def project(head, carry):
        rows = pl.ds(pl.multiple_of(head * TOK, TOK), TOK)
        cols = pl.ds(pl.multiple_of(lax.div(head, 2) * 2 * ROPE, 2 * ROPE), 2 * ROPE)
        q_all[rows, :LATENT] = nn(q[head], wk[head]).astype(BF16)
        keep = (lane < ROPE) == (lax.rem(head, 2) == 0)
        q_all[rows, LATENT:] = jnp.where(keep, q_rope[:, cols], jnp.zeros((), BF16))
        gt_all[:, rows] = nt(wv[head], og[head]).astype(BF16)
        return carry

    lax.fori_loop(0, HEADS, project, 0)

    query_pos = me * TOK + iota((1, TOK), 1)
    doc_start = jnp.zeros((1, TOK), jnp.int32)
    begin = jnp.int32(0)
    for doc in range(lengths.shape[0]):
        end = begin + lengths[doc]
        inside = (query_pos >= begin) & (query_pos < end)
        doc_start = doc_start + jnp.where(inside, begin, 0)
        begin = end
    for block in range(SPAN + 1):
        key_pos = (me - SPAN + block) * TOK + iota((TOK, TOK), 0)
        allowed = (key_pos >= doc_start) & (key_pos <= query_pos)
        bias[block * TOK : (block + 1) * TOK, :] = jnp.where(allowed, 0.0, -jnp.inf).astype(F32)

    for copy in ahead:
        copy.wait_recv()
    around = [
        remote(
            kall.at[pl.ds(0, 3), core, y],
            kall.at[pl.ds(0, 3), core, y],
            yag_s.at[step - 1],
            yag_r.at[step - 1],
            place(y_=up(y, step)),
        )
        for step in (1, 2, 3)
    ]
    for copy in around:
        copy.start()
    for copy in around:
        copy.wait_recv()
    across = remote(kall.at[pl.ds(0, 3), core], kall.at[pl.ds(0, 3), core], sib_s, sib_r, sibling)
    across.start()
    own.wait_recv()
    across.wait_recv()

    for block in range(SPAN + 1):
        at = core + block
        keys = kall[lax.div(at, 2), lax.rem(at, 2)].reshape(TOK, WIDE)
        kw[block * TOK : (block + 1) * TOK, :] = keys
        kwt[:, block * TOK : (block + 1) * TOK] = keys.T

    row, col = iota((NOPE, NOPE), 0), iota((NOPE, NOPE), 1)
    owner = ((row >> 4) & 3) * 32 + ((row >> 2) & 3) * 8 + (row >> 6) * 4 + (row & 3)
    by_owner = (col == owner).astype(F32).astype(BF16)
    eye = (col == row).astype(F32).astype(BF16)
    row, col = iota((64, 64), 0), iota((64, 64), 1)
    by_z = (col == ((row >> 2) & 3) * 16 + (row >> 4) * 4 + (row & 3)).astype(F32).astype(BF16)

    def w_stage0(g):
        return remote(w_out.at[g, other], w_r0.at[g], w0_s.at[g], w0_r.at[g], sibling)

    def w_stage1(g):
        return (
            remote(
                w_out.at[g, core, x_far, pl.ds(0, 64)],
                w_r1.at[g, 0],
                w1_s.at[g, 0],
                w1_r.at[g, 0],
                place(x_=x_next),
            ),
            remote(
                w_out.at[g, core, x_far, pl.ds(64, 64)],
                w_r1.at[g, 1],
                w1_s.at[g, 1],
                w1_r.at[g, 1],
                place(x_=x_prev),
            ),
        )

    def w_stage2(g):
        return (
            remote(
                w_out.at[g, core, x_next],
                w_r2.at[g, 0],
                w2_s.at[g, 0],
                w2_r.at[g, 0],
                place(x_=x_next),
            ),
            remote(
                w_out.at[g, core, x_prev],
                w_r2.at[g, 1],
                w2_s.at[g, 1],
                w2_r.at[g, 1],
                place(x_=x_prev),
            ),
        )

    def w_stage3(g):
        return [
            remote(
                w_v.at[g, up(z, step)],
                w_rz.at[g, step - 1],
                wz_s.at[g, step - 1],
                wz_r.at[g, step - 1],
                place(z_=up(z, step)),
            )
            for step in (1, 2, 3)
        ]

    def w_do1(g):
        w_stage0(g).wait_recv()

        def one(part, carry):
            w_out[g, core, part] = add(w_out[g, core, part], w_r0[g, part]).astype(BF16)
            return carry

        lax.fori_loop(0, 4, one, 0)
        for copy in w_stage1(g):
            copy.start()

    def w_do2(g):
        first, second = w_stage1(g)
        first.wait_recv()
        low = w_out[g, core, x_next, 0:64, :]
        w_out[g, core, x_next, 0:64, :] = add(low, w_r1[g, 0]).astype(BF16)
        second.wait_recv()
        high = w_out[g, core, x_prev, 64:128, :]
        w_out[g, core, x_prev, 64:128, :] = add(high, w_r1[g, 1]).astype(BF16)
        for copy in w_stage2(g):
            copy.start()

    def w_do3(g):
        for copy in w_stage2(g):
            copy.wait_recv()
        total = add(w_out[g, core, x], w_r2[g, 0], w_r2[g, 1]).astype(BF16)
        sorted_keys = nn(by_z, total[0:64, :]).astype(BF16)
        for part in range(4):
            w_v[g, part, 0:16, :] = sorted_keys[part * 16 : part * 16 + 16, :]
            for head in range(PACK):
                w_v[g, part, 16:32, head * 128 : head * 128 + 128] = total[
                    64 + head * 16 : 80 + head * 16, part * 128 : part * 128 + 128
                ]
        for copy in w_stage3(g):
            copy.start()

    def w_do4(g):
        for copy in w_stage3(g):
            copy.wait_recv()
        total = add(w_v[g, z], w_rz[g, 0], w_rz[g, 1], w_rz[g, 2]).astype(BF16)
        g_wk[pl.ds(pl.multiple_of(g * 16, 16), 16), :] = total[0:16, :]
        for head in range(PACK):
            g_wv[g * PACK + head] = total[16:32, head * 128 : head * 128 + 128]

    def group(g, carry):
        cols = pl.ds(pl.multiple_of(g * COLS, COLS), COLS)
        s_buf[...] = nt(kw[...], q_all[cols, :])
        high = jnp.full((1, COLS), -jnp.inf, F32)
        for block in range(SPAN + 1):
            rows = slice(block * TOK, (block + 1) * TOK)
            part = s_buf[rows, :] * SCALE + jnp.concatenate([bias[rows, :]] * PACK, axis=1)
            s_buf[rows, :] = part
            high = jnp.maximum(high, jnp.max(part, axis=0, keepdims=True))
        total = jnp.zeros((1, COLS), F32)
        for block in range(SPAN + 1):
            rows = slice(block * TOK, (block + 1) * TOK)
            part = jnp.exp(s_buf[rows, :] - high)
            s_buf[rows, :] = part
            total = total + jnp.sum(part, axis=0, keepdims=True)
        share = 1.0 / total
        for block in range(SPAN + 1):
            rows = slice(block * TOK, (block + 1) * TOK)
            part = s_buf[rows, :] * share
            s_buf[rows, :] = part
            p_all[rows, cols] = part.astype(BF16)

        @pl.when(g > 0)
        def _():
            w_do1(g - 1)

        gp_buf[...] = nn(kw[:, :LATENT], gt_all[:, cols])
        out_t = nn(kwt[:LATENT, :], p_all[:, cols]).astype(BF16)
        correction = jnp.sum(out_t.astype(F32) * gt_all[:, cols].astype(F32), axis=0, keepdims=True)
        for block in range(SPAN + 1):
            rows = slice(block * TOK, (block + 1) * TOK)
            part = SCALE * s_buf[rows, :] * (gp_buf[rows, :] - correction)
            ds_all[rows, cols] = part.astype(BF16)

        @pl.when(g > 0)
        def _():
            w_do2(g - 1)

        dq_t = nn(kwt[...], ds_all[:, cols]).astype(BF16)
        for local in range(PACK):
            head = g * PACK + local
            here = slice(local * TOK, (local + 1) * TOK)
            mine = dq_t[:LATENT, here]
            gq[head] = nt(eye, nn(wk[head], mine).astype(BF16)).astype(BF16)
            turned = nt(by_owner, q[head]).astype(BF16)
            gwk = nt(turned, mine).astype(BF16)
            gwv = nn(out_t[:, here], og[head]).astype(BF16)
            rows = slice(local * 16, local * 16 + 16)
            more = slice(64 + local * 16, 80 + local * 16)
            for half in range(2):
                for part in range(4):
                    begin = half * 64 + part * 16
                    w_out[g, half, part, rows, :] = gwk[begin : begin + 16, :]
                    for depth in range(4):
                        begin = ((part * 4 + depth) * 2 + half) * 16
                        w_out[g, half, part, more, depth * 128 : depth * 128 + 128] = gwv[
                            begin : begin + 16, :
                        ]
        for pair in range(PACK // 2):
            left = dq_t[LATENT : LATENT + ROPE, pair * 256 : pair * 256 + 128]
            right = dq_t[LATENT + ROPE :, pair * 256 + 128 : pair * 256 + 256]
            both = nt(eye, jnp.concatenate([left, right], axis=0)).astype(BF16)
            at = pl.multiple_of((g * 2 + pair) * 128, 128)
            gq_rope[:, pl.ds(at, 128)] = both
        w_stage0(g).start()

        @pl.when(g > 0)
        def _():
            w_do3(g - 1)

        return carry

    lax.fori_loop(0, GROUPS, group, 0)
    last = GROUPS - 1

    dk[...] = nn(ds_all[...], q_all[...])
    w_do1(last)
    dk[:, :LATENT] = dk[:, :LATENT] + nt(p_all[...], gt_all[...])
    for half in range(2):
        for quarter in range(4):
            for block in range(SPAN + 1):
                begin = block * TOK + quarter * 32 + half * 16
                kg[half, quarter, core + block] = dk[begin : begin + 16, :].astype(BF16)
            kg[half, quarter, 7 * other] = jnp.zeros((16, WIDE), BF16)
    e0 = remote(kg.at[other], k_r0, e0_s, e0_r, sibling)
    e0.start()
    w_do2(last)
    e0.wait_recv()
    for quarter in range(4):
        kg[core, quarter] = add(kg[core, quarter], k_r0[quarter]).astype(BF16)
    e1 = (
        remote(
            kg.at[core, y_far, pl.ds(0, 4)], k_r1.at[0], e1_s.at[0], e1_r.at[0], place(y_=y_next)
        ),
        remote(
            kg.at[core, y_far, pl.ds(4, 4)], k_r1.at[1], e1_s.at[1], e1_r.at[1], place(y_=y_prev)
        ),
    )
    for copy in e1:
        copy.start()
    for copy in e1:
        copy.wait_recv()
    low = kg[core, y_next, 0:4]
    kg[core, y_next, 0:4] = add(low, k_r1[0]).astype(BF16)
    high = kg[core, y_prev, 4:8]
    kg[core, y_prev, 4:8] = add(high, k_r1[1]).astype(BF16)
    e2 = (
        remote(kg.at[core, y_next], k_r2.at[0], e2_s.at[0], e2_r.at[0], place(y_=y_next)),
        remote(kg.at[core, y_prev], k_r2.at[1], e2_s.at[1], e2_r.at[1], place(y_=y_prev)),
    )
    for copy in e2:
        copy.start()
    w_do3(last)
    for copy in e2:
        copy.wait_recv()
    k_sum[...] = add(kg[core, y], k_r2[0], k_r2[1]).astype(BF16)
    e3 = [
        remote(
            k_sum.at[pl.ds((3 - step) * 2, 2)],
            k_r3.at[step - 1],
            e3_s.at[step - 1],
            e3_r.at[step - 1],
            chip_at(-step),
        )
        for step in (1, 2, 3)
    ]
    for copy in e3:
        copy.start()
    for g in range(last):
        w_do4(g)
    for copy in e3:
        copy.wait_recv()
    k_mid[...] = add(k_sum[6:8], k_r3[0], k_r3[1], k_r3[2]).astype(BF16)
    e4 = remote(k_mid, k_r4, e4_s, e4_r, place(zh_=1 - zh))
    e4.start()
    w_do4(last)
    e4.wait_recv()
    total = add(k_mid[...], k_r4[...])
    k_fin[:, :, :LATENT] = total[:, :, :LATENT].astype(BF16)
    rope_part = total[:, :, LATENT:].reshape(32, 2 * ROPE)
    rope_part = rope_part + pltpu.roll(rope_part, ROPE, 1)
    k_fin[:, :, LATENT:] = rope_part.reshape(2, 16, 2 * ROPE).astype(BF16)
    k_out[y, core] = k_fin[core]
    e5 = [
        remote(
            k_fin.at[core],
            k_out.at[y, core],
            e5_s.at[step - 1],
            e5_r.at[step - 1],
            place(y_=up(y, step)),
        )
        for step in (1, 2, 3)
    ] + [
        remote(
            k_fin.at[other],
            k_out.at[y, core],
            e5_s.at[3 + step],
            e5_r.at[3 + step],
            place(y_=up(y, step), core_=other),
        )
        for step in (0, 1, 2, 3)
    ]
    for copy in e5:
        copy.start()
    for copy in e5:
        copy.wait_recv()
    for quarter in range(4):
        for half in range(2):
            begin = quarter * 32 + half * 16
            g_latent[begin : begin + 16, :] = k_out[quarter, half, :, :LATENT]
            g_rope[begin : begin + 16, :] = k_out[quarter, half, :, LATENT : LATENT + ROPE]

    own.wait_send()
    across.wait_send()
    e0.wait_send()
    e4.wait_send()
    for copy in [*ahead, *around, *e1, *e2, *e3, *e5]:
        copy.wait_send()
    for g in range(GROUPS):
        for copy in [w_stage0(g), *w_stage1(g), *w_stage2(g), *w_stage3(g)]:
            copy.wait_send()


def per_device(q_nope, q_rope, latent, k_rope, out_grad, w_key, w_value, lengths):
    dma = pltpu.SemaphoreType.DMA
    vmem = pl.BlockSpec(memory_space=pltpu.VMEM)

    def held(*shape, dtype=BF16):
        return pltpu.VMEM(shape, dtype)

    out = pl.pallas_call(
        kernel,
        out_shape=(
            jax.ShapeDtypeStruct((HEADS, TOK, NOPE), BF16),
            jax.ShapeDtypeStruct((TOK, HEADS * ROPE), BF16),
            jax.ShapeDtypeStruct((TOK, LATENT), BF16),
            jax.ShapeDtypeStruct((TOK, ROPE), BF16),
            jax.ShapeDtypeStruct((HEADS * 4, LATENT), BF16),
            jax.ShapeDtypeStruct((HEADS, 16, NOPE), BF16),
        ),
        in_specs=[pl.BlockSpec(memory_space=pltpu.SMEM)] + [vmem] * 7,
        out_specs=[vmem] * 6,
        scratch_shapes=[
            held(4, 2, 4, 32, WIDE),
            held(WINDOW, WIDE),
            held(WIDE, WINDOW),
            held(HEADS * TOK, WIDE),
            held(LATENT, HEADS * TOK),
            held(WINDOW, HEADS * TOK),
            held(WINDOW, HEADS * TOK),
            held(WINDOW, COLS, dtype=F32),
            held(WINDOW, COLS, dtype=F32),
            held(WINDOW, TOK, dtype=F32),
            held(WINDOW, WIDE, dtype=F32),
            held(GROUPS, 2, 4, 128, LATENT),
            held(GROUPS, 4, 128, LATENT),
            held(GROUPS, 2, 64, LATENT),
            held(GROUPS, 2, 128, LATENT),
            held(GROUPS, 4, 32, LATENT),
            held(GROUPS, 3, 32, LATENT),
            held(2, 4, 8, 16, WIDE),
            held(4, 8, 16, WIDE),
            held(2, 4, 16, WIDE),
            held(2, 8, 16, WIDE),
            held(8, 16, WIDE),
            held(3, 2, 16, WIDE),
            held(2, 16, WIDE),
            held(2, 16, WIDE),
            held(2, 16, WIDE),
            held(4, 2, 16, WIDE),
            dma,
            dma,
            dma((3,)),
            dma((3,)),
            dma((3,)),
            dma((3,)),
            dma,
            dma,
            dma((GROUPS,)),
            dma((GROUPS,)),
            dma((GROUPS, 2)),
            dma((GROUPS, 2)),
            dma((GROUPS, 2)),
            dma((GROUPS, 2)),
            dma((GROUPS, 3)),
            dma((GROUPS, 3)),
            dma,
            dma,
            dma((2,)),
            dma((2,)),
            dma((2,)),
            dma((2,)),
            dma((3,)),
            dma((3,)),
            dma,
            dma,
            dma((7,)),
            dma((7,)),
        ],
        compiler_params=pltpu.CompilerParams(
            collective_id=0, has_side_effects=True, vmem_limit_bytes=58 * 2**20
        ),
        cost_estimate=pl.CostEstimate(
            flops=15 * 10**9, bytes_accessed=8 * 10**6, transcendentals=2 * 10**6
        ),
        name="mla_backward",
    )(
        lengths,
        q_nope.transpose(1, 0, 2),
        q_rope,
        latent,
        k_rope,
        out_grad.transpose(1, 0, 2),
        w_key,
        w_value,
    )
    gq, gq_rope, g_latent, g_rope, g_wk, g_wv = out
    return (
        gq.transpose(1, 0, 2),
        gq_rope,
        g_latent,
        g_rope,
        g_wk.reshape(HEADS, 4, LATENT),
        g_wv,
    )


def solution(mesh):
    placed = (
        P("ctx", "tp", None),
        P("ctx", "tp"),
        P("ctx", None),
        P("ctx", None),
        P("ctx", "tp", None),
        P("tp", None, None),
        P("tp", None, None),
        P(),
    )
    return jax.shard_map(
        per_device,
        mesh=mesh,
        in_specs=placed,
        out_specs=(
            P("ctx", "tp", None),
            P("ctx", "tp"),
            P("ctx", None),
            P("ctx", None),
            P("tp", "ctx", None),
            P("tp", "ctx", None),
        ),
        check_vma=False,
    )
```

```python
import jax
import jax.numpy as jnp
from jax import lax
from jax.experimental import pallas as pl
from jax.experimental.pallas import tpu as pltpu
from jax.sharding import PartitionSpec as P

NOPE = 128
ROPE = 64
LATENT = 512
WIDE = LATENT + 2 * ROPE
TOK = 128
SPAN = 6
WINDOW = (SPAN + 1) * TOK
HEADS = 16
PACK = 4
GROUPS = HEADS // PACK
JOBS = 2 * GROUPS
COLS = PACK * TOK
SCALE = float(NOPE + ROPE) ** -0.5
MESH = pl.DeviceIdType.MESH
F32 = jnp.float32
BF16 = jnp.bfloat16


def nn(a, b):
    return lax.dot_general(a, b, (((1,), (0,)), ((), ())), preferred_element_type=F32)


def nt(a, b):
    return lax.dot_general(a, b, (((1,), (1,)), ((), ())), preferred_element_type=F32)


def add(*terms):
    total = terms[0].astype(F32)
    for term in terms[1:]:
        total = total + term.astype(F32)
    return total


def iota(shape, dim):
    return lax.broadcasted_iota(jnp.int32, shape, dim)


def kernel(
    lengths,
    q_hbm,
    qr_hbm,
    latent,
    rope_t,
    og_hbm,
    wk_hbm,
    wv_hbm,
    gq,
    gq_rope,
    g_latent,
    g_rope_t,
    g_wk,
    g_wv,
    q_in,
    og_in,
    q_rope,
    wk,
    wv,
    og,
    qt,
    gq_t,
    kall,
    kw,
    kwt,
    q_all,
    gt_all,
    p_all,
    ds_all,
    s_buf,
    gp_buf,
    bias,
    w_out,
    w_r0,
    w_r1,
    w_r2,
    w_v,
    w_rz,
    kg,
    k_r0,
    k_r1,
    k_r2,
    k_sum,
    k_r3,
    k_mid,
    k_r4,
    k_fin,
    k_out,
    load_s,
    own_s,
    own_r,
    ctx_s,
    ctx_r,
    yag_s,
    yag_r,
    sib_s,
    sib_r,
    w0_s,
    w0_r,
    w1_s,
    w1_r,
    w2_s,
    w2_r,
    wz_s,
    wz_r,
    e0_s,
    e0_r,
    e1_s,
    e1_r,
    e2_s,
    e2_r,
    e3_s,
    e3_r,
    e4_s,
    e4_r,
    e5_s,
    e5_r,
):
    me = lax.axis_index("ctx")
    tp = lax.axis_index("tp")
    core = lax.rem(me, 2)
    chip = lax.div(me, 2)
    z = lax.rem(chip, 4)
    x = lax.div(chip, 4)
    y = lax.rem(tp, 4)
    zh = lax.div(tp, 4)
    other = 1 - core

    def place(x_=x, z_=z, core_=core, y_=y, zh_=zh):
        return ((x_ * 4 + z_) * 2 + core_, zh_ * 4 + y_)

    def up(value, step):
        return lax.rem(value + step, 4)

    def chip_at(step):
        return (lax.rem(chip + step + 16, 16) * 2 + core, tp)

    sibling = place(core_=other)
    x_next, x_prev, x_far = up(x, 1), up(x, 3), up(x, 2)
    y_next, y_prev, y_far = up(y, 1), up(y, 3), up(y, 2)

    barrier = pltpu.get_barrier_semaphore()
    peers = [sibling, place(x_=x_next), place(x_=x_prev), place(zh_=1 - zh)]
    for step in (1, 2, 3):
        peers += [place(z_=up(z, step)), chip_at(step), chip_at(-step)]
        peers += [place(y_=up(y, step)), place(y_=up(y, step), core_=other)]
    for peer in peers:
        pl.semaphore_signal(barrier, inc=1, device_id=peer, device_id_type=MESH)

    loads = [
        pltpu.make_async_copy(src, dst, load_s.at[n])
        for n, (src, dst) in enumerate(
            [(q_hbm, q_in), (wk_hbm, wk), (og_hbm, og_in), (wv_hbm, wv), (qr_hbm, q_rope)]
        )
    ]
    for copy in loads:
        copy.start()

    def remote(src, dst, send, recv, peer):
        return pltpu.make_async_remote_copy(
            src_ref=src,
            dst_ref=dst,
            send_sem=send,
            recv_sem=recv,
            device_id=peer,
            device_id_type=MESH,
        )

    rope = rope_t[...].T
    rope = jnp.concatenate([rope, rope], axis=1)
    for quarter in range(4):
        rows = slice(quarter * 32, quarter * 32 + 32)
        kall[3, core, quarter, :, :LATENT] = latent[rows, :]
        kall[3, core, quarter, :, LATENT:] = rope[rows, :]
    pl.semaphore_wait(barrier, len(peers))

    own = remote(kall.at[3, core], kall.at[3, core], own_s, own_r, sibling)
    ahead = [
        remote(
            kall.at[3, core, y],
            kall.at[3 - step, core, y],
            ctx_s.at[step - 1],
            ctx_r.at[step - 1],
            chip_at(step),
        )
        for step in (1, 2, 3)
    ]
    for copy in ahead:
        copy.start()
    own.start()

    row, col = iota((NOPE, NOPE), 0), iota((NOPE, NOPE), 1)
    owner = ((row >> 4) & 3) * 32 + ((row >> 2) & 3) * 8 + (row >> 6) * 4 + (row & 3)
    by_owner = (col == owner).astype(F32).astype(BF16)
    eye = (col == row).astype(F32).astype(BF16)
    row, col = iota((64, 64), 0), iota((64, 64), 1)
    by_z = (col == ((row >> 2) & 3) * 16 + (row >> 4) * 4 + (row & 3)).astype(F32).astype(BF16)

    lane = iota((TOK, 2 * ROPE), 1)

    def project(head, carry):
        rows = pl.ds(pl.multiple_of(head * TOK, TOK), TOK)
        cols = pl.ds(pl.multiple_of(lax.div(head, 2) * 2 * ROPE, 2 * ROPE), 2 * ROPE)
        mine = gq_t[head]
        q_all[rows, :LATENT] = nn(mine, wk[head]).astype(BF16)
        keep = (lane < ROPE) == (lax.rem(head, 2) == 0)
        q_all[rows, LATENT:] = jnp.where(keep, q_rope[:, cols], jnp.zeros((), BF16))
        qt[head] = nt(by_owner, mine).astype(BF16)
        gt_all[:, rows] = nt(wv[head], og[head]).astype(BF16)
        return carry

    for copy in loads:
        copy.wait()
    gq_t[...] = jnp.swapaxes(q_in[...], 0, 1)
    og[...] = jnp.swapaxes(og_in[...], 0, 1)
    lax.fori_loop(0, HEADS // 2, project, 0)

    around = []
    for near in (1, 2, 3):
        ahead[near - 1].wait_recv()
        part = kall.at[3 - near, core, y]
        around.append(
            [
                remote(
                    part,
                    part,
                    yag_s.at[near - 1, step - 1],
                    yag_r.at[near - 1, step - 1],
                    place(y_=up(y, step)),
                )
                for step in (1, 2, 3)
            ]
        )
        for copy in around[-1]:
            copy.start()

    lax.fori_loop(HEADS // 2, HEADS, project, 0)

    query_pos = me * TOK + iota((1, TOK), 1)
    doc_start = jnp.zeros((1, TOK), jnp.int32)
    begin = jnp.int32(0)
    for doc in range(lengths.shape[0]):
        end = begin + lengths[doc]
        inside = (query_pos >= begin) & (query_pos < end)
        doc_start = doc_start + jnp.where(inside, begin, 0)
        begin = end
    for block in range(SPAN + 1):
        key_pos = (me - SPAN + block) * TOK + iota((TOK, TOK), 0)
        allowed = (key_pos >= doc_start) & (key_pos <= query_pos)
        bias[block * TOK : (block + 1) * TOK, :] = jnp.where(allowed, 0.0, -jnp.inf).astype(F32)

    across = []
    for near in (1, 2, 3):
        for copy in around[near - 1]:
            copy.wait_recv()
        part = kall.at[3 - near, core]
        across.append(remote(part, part, sib_s.at[near - 1], sib_r.at[near - 1], sibling))
        across[-1].start()
    own.wait_recv()
    for copy in across:
        copy.wait_recv()

    for block in range(SPAN + 1):
        at = core + block
        keys = kall[lax.div(at, 2), lax.rem(at, 2)].reshape(TOK, WIDE)
        kw[block * TOK : (block + 1) * TOK, :] = keys
        kwt[:, block * TOK : (block + 1) * TOK] = keys.T

    def w_stage0(g):
        return remote(w_out.at[g, other], w_r0.at[g], w0_s.at[g], w0_r.at[g], sibling)

    def w_stage1(g):
        return (
            remote(
                w_out.at[g, core, x_far, pl.ds(0, 32)],
                w_r1.at[g, 0],
                w1_s.at[g, 0],
                w1_r.at[g, 0],
                place(x_=x_next),
            ),
            remote(
                w_out.at[g, core, x_far, pl.ds(32, 32)],
                w_r1.at[g, 1],
                w1_s.at[g, 1],
                w1_r.at[g, 1],
                place(x_=x_prev),
            ),
        )

    def w_stage2(g):
        return (
            remote(
                w_out.at[g, core, x_next],
                w_r2.at[g, 0],
                w2_s.at[g, 0],
                w2_r.at[g, 0],
                place(x_=x_next),
            ),
            remote(
                w_out.at[g, core, x_prev],
                w_r2.at[g, 1],
                w2_s.at[g, 1],
                w2_r.at[g, 1],
                place(x_=x_prev),
            ),
        )

    def w_stage3(g):
        return [
            remote(
                w_v.at[g, up(z, step)],
                w_rz.at[g, step - 1],
                wz_s.at[g, step - 1],
                wz_r.at[g, step - 1],
                place(z_=up(z, step)),
            )
            for step in (1, 2, 3)
        ]

    def w_do1(g):
        w_stage0(g).wait_recv()

        def one(part, carry):
            w_out[g, core, part] = add(w_out[g, core, part], w_r0[g, part]).astype(BF16)
            return carry

        lax.fori_loop(0, 4, one, 0)
        for copy in w_stage1(g):
            copy.start()

    def w_do2(g):
        first, second = w_stage1(g)
        first.wait_recv()
        low = w_out[g, core, x_next, 0:32, :]
        w_out[g, core, x_next, 0:32, :] = add(low, w_r1[g, 0]).astype(BF16)
        second.wait_recv()
        high = w_out[g, core, x_prev, 32:64, :]
        w_out[g, core, x_prev, 32:64, :] = add(high, w_r1[g, 1]).astype(BF16)
        for copy in w_stage2(g):
            copy.start()

    def w_do3(g, of_key):
        for copy in w_stage2(g):
            copy.wait_recv()
        total = add(w_out[g, core, x], w_r2[g, 0], w_r2[g, 1]).astype(BF16)
        if of_key:
            total = nn(by_z, total).astype(BF16)
            for part in range(4):
                w_v[g, part] = total[part * 16 : part * 16 + 16, :]
        else:
            for part in range(4):
                for head in range(PACK):
                    w_v[g, part, :, head * 128 : head * 128 + 128] = total[
                        head * 16 : head * 16 + 16, part * 128 : part * 128 + 128
                    ]
        for copy in w_stage3(g):
            copy.start()

    def w_do4(g, of_key):
        for copy in w_stage3(g):
            copy.wait_recv()
        total = add(w_v[g, z], w_rz[g, 0], w_rz[g, 1], w_rz[g, 2]).astype(BF16)
        for local in range(PACK):
            if of_key:
                g_wk[(g - GROUPS) * PACK + local] = total[local * 4 : local * 4 + 4, :]
            else:
                g_wv[g * PACK + local] = total[:, local * 128 : local * 128 + 128]

    def group(g, carry):
        cols = pl.ds(pl.multiple_of(g * COLS, COLS), COLS)
        s_buf[...] = nt(kw[...], q_all[cols, :])
        @pl.when(g > 0)
        def _():
            w_do1(g - 1)

        high = jnp.full((1, COLS), -jnp.inf, F32)
        for block in range(SPAN + 1):
            rows = slice(block * TOK, (block + 1) * TOK)
            part = s_buf[rows, :] * SCALE + jnp.concatenate([bias[rows, :]] * PACK, axis=1)
            s_buf[rows, :] = part
            high = jnp.maximum(high, jnp.max(part, axis=0, keepdims=True))
        total = jnp.zeros((1, COLS), F32)
        for block in range(SPAN + 1):
            rows = slice(block * TOK, (block + 1) * TOK)
            part = jnp.exp(s_buf[rows, :] - high)
            s_buf[rows, :] = part
            total = total + jnp.sum(part, axis=0, keepdims=True)
        share = 1.0 / total
        for block in range(SPAN + 1):
            rows = slice(block * TOK, (block + 1) * TOK)
            part = s_buf[rows, :] * share
            s_buf[rows, :] = part
            p_all[rows, cols] = part.astype(BF16)

        @pl.when(g > 0)
        def _():
            w_do2(g - 1)

        gp_buf[...] = nn(kw[:, :LATENT], gt_all[:, cols])
        out_t = nn(kwt[:LATENT, :], p_all[:, cols]).astype(BF16)
        correction = jnp.sum(out_t.astype(F32) * gt_all[:, cols].astype(F32), axis=0, keepdims=True)
        for block in range(SPAN + 1):
            rows = slice(block * TOK, (block + 1) * TOK)
            part = SCALE * s_buf[rows, :] * (gp_buf[rows, :] - correction)
            ds_all[rows, cols] = part.astype(BF16)

        for local in range(PACK):
            gwv = nn(out_t[:, local * TOK : (local + 1) * TOK], og[g * PACK + local]).astype(BF16)
            rows = slice(local * 16, local * 16 + 16)
            for half in range(2):
                for part in range(4):
                    for depth in range(4):
                        begin = ((part * 4 + depth) * 2 + half) * 16
                        w_out[g, half, part, rows, depth * 128 : depth * 128 + 128] = gwv[
                            begin : begin + 16, :
                        ]
        w_stage0(g).start()

        @pl.when(g > 0)
        def _():
            w_do3(g - 1, False)

        return carry

    def second(g):
        cols = slice(g * COLS, (g + 1) * COLS)
        dq_t = nn(kwt[...], ds_all[:, cols]).astype(BF16)
        for local in range(PACK):
            head = g * PACK + local
            here = slice(local * TOK, (local + 1) * TOK)
            mine = dq_t[:LATENT, here]
            gq_t[head] = nt(eye, nn(wk[head], mine).astype(BF16)).astype(BF16)
            gwk = nt(qt[head], mine).astype(BF16)
            rows = slice(local * 16, local * 16 + 16)
            for half in range(2):
                for part in range(4):
                    begin = half * 64 + part * 16
                    w_out[GROUPS + g, half, part, rows, :] = gwk[begin : begin + 16, :]
        for pair in range(PACK // 2):
            left = dq_t[LATENT : LATENT + ROPE, pair * 256 : pair * 256 + 128]
            right = dq_t[LATENT + ROPE :, pair * 256 + 128 : pair * 256 + 256]
            both = nt(eye, jnp.concatenate([left, right], axis=0)).astype(BF16)
            gq_rope[:, (g * 2 + pair) * 128 : (g * 2 + pair + 1) * 128] = both
        w_stage0(GROUPS + g).start()

    lax.fori_loop(0, GROUPS, group, 0)
    last = GROUPS - 1

    def key_terms(first, after):
        rows = slice(first * TOK, after * TOK)
        wide = nn(ds_all[rows, :], q_all[...])
        narrow = wide[:, :LATENT] + nt(p_all[rows, :], gt_all[...])
        narrow, side = narrow.astype(BF16), wide[:, LATENT:].astype(BF16)
        for block in range(first, after):
            for quarter in range(4):
                for half in range(2):
                    begin = (block - first) * TOK + quarter * 32 + half * 16
                    kg[half, quarter, core + block, :, :LATENT] = narrow[begin : begin + 16, :]
                    kg[half, quarter, core + block, :, LATENT:] = side[begin : begin + 16, :]

    def e0(n):
        blocks = pl.ds(4 * n, 4)
        return remote(
            kg.at[other, :, blocks], k_r0.at[:, blocks], e0_s.at[n], e0_r.at[n], sibling
        )

    def e1(n):
        return [
            remote(
                kg.at[core, y_far, pl.ds(4 * n + 2 * way, 2)],
                k_r1.at[n, way],
                e1_s.at[n, way],
                e1_r.at[n, way],
                place(y_=y_to),
            )
            for way, y_to in ((0, y_next), (1, y_prev))
        ]

    def e2(n):
        return [
            remote(
                kg.at[core, y_to, pl.ds(4 * n, 4)],
                k_r2.at[n, way],
                e2_s.at[n, way],
                e2_r.at[n, way],
                place(y_=y_to),
            )
            for way, y_to in ((0, y_next), (1, y_prev))
        ]

    def e3(step):
        return remote(
            k_sum.at[pl.ds((3 - step) * 2, 2)],
            k_r3.at[step - 1],
            e3_s.at[step - 1],
            e3_r.at[step - 1],
            chip_at(-step),
        )

    def k_do1(n):
        e0(n).wait_recv()
        blocks = slice(4 * n, 4 * n + 4)
        for quarter in range(4):
            kg[core, quarter, blocks] = add(kg[core, quarter, blocks], k_r0[quarter, blocks]).astype(
                BF16
            )
        for copy in e1(n):
            copy.start()

    def k_do2(n):
        for way, (copy, y_to) in enumerate(zip(e1(n), (y_next, y_prev))):
            copy.wait_recv()
            blocks = slice(4 * n + 2 * way, 4 * n + 2 * way + 2)
            kg[core, y_to, blocks] = add(kg[core, y_to, blocks], k_r1[n, way]).astype(BF16)
        for copy in e2(n):
            copy.start()

    def k_do3(n):
        for copy in e2(n):
            copy.wait_recv()
        blocks = slice(4 * n, 4 * n + 4)
        k_sum[blocks] = add(kg[core, y, blocks], k_r2[n, 0], k_r2[n, 1]).astype(BF16)
        for step in ((3, 2), (1,))[n]:
            e3(step).start()

    for half in range(2):
        for quarter in range(4):
            kg[half, quarter, 7 * other] = jnp.zeros((16, WIDE), BF16)
    w_do1(last)
    key_terms(0, 4)
    e0(0).start()
    w_do2(last)
    key_terms(4, 7)
    e0(1).start()
    k_do1(0)
    second(0)
    k_do1(1)
    w_do3(last, False)
    k_do2(0)
    second(1)
    k_do2(1)
    k_do3(0)
    w_do1(GROUPS)
    second(2)
    k_do3(1)
    w_do2(GROUPS)
    w_do1(GROUPS + 1)
    second(3)
    for step in (1, 2, 3):
        e3(step).wait_recv()
    k_mid[...] = add(k_sum[6:8], k_r3[0], k_r3[1], k_r3[2]).astype(BF16)
    e4 = remote(k_mid, k_r4, e4_s, e4_r, place(zh_=1 - zh))
    e4.start()
    w_do3(GROUPS, True)
    w_do2(GROUPS + 1)
    w_do1(GROUPS + 2)
    w_do1(GROUPS + 3)
    gq[...] = jnp.swapaxes(gq_t[...], 0, 1)
    e4.wait_recv()
    total = add(k_mid[...], k_r4[...])
    k_fin[:, :, :LATENT] = total[:, :, :LATENT].astype(BF16)
    rope_part = total[:, :, LATENT:].reshape(32, 2 * ROPE)
    rope_part = rope_part + pltpu.roll(rope_part, ROPE, 1)
    k_fin[:, :, LATENT:] = rope_part.reshape(2, 16, 2 * ROPE).astype(BF16)
    k_out[y, core] = k_fin[core]
    e5 = [
        remote(
            k_fin.at[core],
            k_out.at[y, core],
            e5_s.at[step - 1],
            e5_r.at[step - 1],
            place(y_=up(y, step)),
        )
        for step in (1, 2, 3)
    ] + [
        remote(
            k_fin.at[other],
            k_out.at[y, core],
            e5_s.at[3 + step],
            e5_r.at[3 + step],
            place(y_=up(y, step), core_=other),
        )
        for step in (0, 1, 2, 3)
    ]
    for copy in e5:
        copy.start()
    w_do3(GROUPS + 1, True)
    w_do2(GROUPS + 2)
    w_do2(GROUPS + 3)
    for g in range(GROUPS):
        w_do4(g, False)
    w_do3(GROUPS + 2, True)
    w_do3(GROUPS + 3, True)
    for copy in e5:
        copy.wait_recv()
    for quarter in range(4):
        for half in range(2):
            begin = quarter * 32 + half * 16
            g_latent[begin : begin + 16, :] = k_out[quarter, half, :, :LATENT]
    g_rope_t[...] = k_out[:, :, :, LATENT:].reshape(TOK, 2 * ROPE).T[:ROPE, :]
    for g in range(GROUPS, JOBS):
        w_do4(g, True)

    own.wait_send()
    e4.wait_send()
    for n in range(2):
        for copy in [e0(n), *e1(n), *e2(n)]:
            copy.wait_send()
    for copy in [*ahead, *across, *e5, *(copy for three in around for copy in three)]:
        copy.wait_send()
    for step in (1, 2, 3):
        e3(step).wait_send()
    for g in range(JOBS):
        for copy in [w_stage0(g), *w_stage1(g), *w_stage2(g), *w_stage3(g)]:
            copy.wait_send()


def hand_over(*refs):
    count = len(refs) // 2
    for source, target in zip(refs[:count], refs[count:]):
        target[...] = source[...]


def per_device(q_nope, q_rope, latent, k_rope, out_grad, w_key, w_value, lengths):
    dma = pltpu.SemaphoreType.DMA
    vmem = pl.BlockSpec(memory_space=pltpu.VMEM)
    hbm = pl.BlockSpec(memory_space=pl.ANY)

    def held(*shape, dtype=BF16):
        return pltpu.VMEM(shape, dtype)

    out = pl.pallas_call(
        kernel,
        out_shape=(
            jax.ShapeDtypeStruct((TOK, HEADS, NOPE), BF16),
            jax.ShapeDtypeStruct((TOK, HEADS * ROPE), BF16),
            jax.ShapeDtypeStruct((TOK, LATENT), BF16),
            jax.ShapeDtypeStruct((ROPE, TOK), BF16),
            jax.ShapeDtypeStruct((HEADS, 4, LATENT), BF16),
            jax.ShapeDtypeStruct((HEADS, 16, NOPE), BF16),
        ),
        in_specs=[pl.BlockSpec(memory_space=pltpu.SMEM), hbm, hbm, vmem, vmem, hbm, hbm, hbm],
        out_specs=[vmem] * 6,
        scratch_shapes=[
            held(TOK, HEADS, NOPE),
            held(TOK, HEADS, NOPE),
            held(TOK, HEADS * ROPE),
            held(HEADS, NOPE, LATENT),
            held(HEADS, LATENT, NOPE),
            held(HEADS, TOK, NOPE),
            held(HEADS, NOPE, TOK),
            held(HEADS, TOK, NOPE),
            held(4, 2, 4, 32, WIDE),
            held(WINDOW, WIDE),
            held(WIDE, WINDOW),
            held(HEADS * TOK, WIDE),
            held(LATENT, HEADS * TOK),
            held(WINDOW, HEADS * TOK),
            held(WINDOW, HEADS * TOK),
            held(WINDOW, COLS, dtype=F32),
            held(WINDOW, COLS, dtype=F32),
            held(WINDOW, TOK, dtype=F32),
            held(JOBS, 2, 4, 64, LATENT),
            held(JOBS, 4, 64, LATENT),
            held(JOBS, 2, 32, LATENT),
            held(JOBS, 2, 64, LATENT),
            held(JOBS, 4, 16, LATENT),
            held(JOBS, 3, 16, LATENT),
            held(2, 4, 8, 16, WIDE),
            held(4, 8, 16, WIDE),
            held(2, 2, 2, 16, WIDE),
            held(2, 2, 4, 16, WIDE),
            held(8, 16, WIDE),
            held(3, 2, 16, WIDE),
            held(2, 16, WIDE),
            held(2, 16, WIDE),
            held(2, 16, WIDE),
            held(4, 2, 16, WIDE),
            dma((5,)),
            dma,
            dma,
            dma((3,)),
            dma((3,)),
            dma((3, 3)),
            dma((3, 3)),
            dma((3,)),
            dma((3,)),
            dma((JOBS,)),
            dma((JOBS,)),
            dma((JOBS, 2)),
            dma((JOBS, 2)),
            dma((JOBS, 2)),
            dma((JOBS, 2)),
            dma((JOBS, 3)),
            dma((JOBS, 3)),
            dma((2,)),
            dma((2,)),
            dma((2, 2)),
            dma((2, 2)),
            dma((2, 2)),
            dma((2, 2)),
            dma((3,)),
            dma((3,)),
            dma,
            dma,
            dma((7,)),
            dma((7,)),
        ],
        compiler_params=pltpu.CompilerParams(
            collective_id=0, has_side_effects=True, vmem_limit_bytes=58 * 2**20
        ),
        cost_estimate=pl.CostEstimate(
            flops=15 * 10**9, bytes_accessed=8 * 10**6, transcendentals=2 * 10**6
        ),
        name="mla_backward",
    )(
        lengths,
        q_nope,
        q_rope,
        latent,
        k_rope.T,
        out_grad,
        w_key,
        w_value,
    )
    gq, gq_rope, g_latent, g_rope_t, g_wk, g_wv = pl.pallas_call(
        hand_over,
        out_shape=tuple(jax.ShapeDtypeStruct(array.shape, array.dtype) for array in out),
        in_specs=[vmem] * len(out),
        out_specs=[vmem] * len(out),
        name="hand_over",
    )(*out)
    return gq, gq_rope, g_latent, g_rope_t.T, g_wk, g_wv


def solution(mesh):
    placed = (
        P("ctx", "tp", None),
        P("ctx", "tp"),
        P("ctx", None),
        P("ctx", None),
        P("ctx", "tp", None),
        P("tp", None, None),
        P("tp", None, None),
        P(),
    )
    return jax.shard_map(
        per_device,
        mesh=mesh,
        in_specs=placed,
        out_specs=(
            P("ctx", "tp", None),
            P("ctx", "tp"),
            P("ctx", None),
            P("ctx", None),
            P("tp", "ctx", None),
            P("tp", "ctx", None),
        ),
        check_vma=False,
    )
```

```python
import jax
import jax.numpy as jnp
from jax import lax
from jax.experimental import pallas as pl
from jax.experimental.pallas import tpu as pltpu
from jax.sharding import PartitionSpec as P

NOPE = 128
ROPE = 64
LATENT = 512
WIDE = LATENT + 2 * ROPE
TOK = 128
SPAN = 6
WINDOW = (SPAN + 1) * TOK
HEADS = 16
PACK = 4
GROUPS = HEADS // PACK
JOBS = 2 * GROUPS
COLS = PACK * TOK
SCALE = float(NOPE + ROPE) ** -0.5
MESH = pl.DeviceIdType.MESH
F32 = jnp.float32
BF16 = jnp.bfloat16


def nn(a, b):
    return lax.dot_general(a, b, (((1,), (0,)), ((), ())), preferred_element_type=F32)


def nt(a, b):
    return lax.dot_general(a, b, (((1,), (1,)), ((), ())), preferred_element_type=F32)


def add(*terms):
    total = terms[0].astype(F32)
    for term in terms[1:]:
        total = total + term.astype(F32)
    return total


def iota(shape, dim):
    return lax.broadcasted_iota(jnp.int32, shape, dim)


def kernel(
    lengths,
    q_hbm,
    qr_hbm,
    latent,
    rope_t,
    og_hbm,
    wk_hbm,
    wv_hbm,
    gq,
    gq_rope,
    g_latent,
    g_rope_t,
    g_wk,
    g_wv,
    q_in,
    og_in,
    q_rope,
    wk,
    wv,
    og,
    qt,
    gq_t,
    kall,
    kw,
    kwt,
    q_all,
    gt_all,
    p_all,
    ds_all,
    s_buf,
    gp_buf,
    bias,
    w_out,
    w_r0,
    w_r1,
    w_r2,
    w_v,
    w_rz,
    kg,
    k_r0,
    k_r1,
    k_r2,
    k_sum,
    k_r3,
    k_mid,
    k_r4,
    k_fin,
    k_out,
    load_s,
    own_s,
    own_r,
    ctx_s,
    ctx_r,
    yag_s,
    yag_r,
    sib_s,
    sib_r,
    w0_s,
    w0_r,
    w1_s,
    w1_r,
    w2_s,
    w2_r,
    wz_s,
    wz_r,
    e0_s,
    e0_r,
    e1_s,
    e1_r,
    e2_s,
    e2_r,
    e3_s,
    e3_r,
    e4_s,
    e4_r,
    e5_s,
    e5_r,
):
    me = lax.axis_index("ctx")
    tp = lax.axis_index("tp")
    core = lax.rem(me, 2)
    chip = lax.div(me, 2)
    z = lax.rem(chip, 4)
    x = lax.div(chip, 4)
    y = lax.rem(tp, 4)
    zh = lax.div(tp, 4)
    other = 1 - core

    def place(x_=x, z_=z, core_=core, y_=y, zh_=zh):
        return ((x_ * 4 + z_) * 2 + core_, zh_ * 4 + y_)

    def up(value, step):
        return lax.rem(value + step, 4)

    def chip_at(step):
        return (lax.rem(chip + step + 16, 16) * 2 + core, tp)

    sibling = place(core_=other)
    x_next, x_prev, x_far = up(x, 1), up(x, 3), up(x, 2)
    y_next, y_prev, y_far = up(y, 1), up(y, 3), up(y, 2)

    barrier = pltpu.get_barrier_semaphore()
    peers = [sibling, place(x_=x_next), place(x_=x_prev), place(zh_=1 - zh)]
    for step in (1, 2, 3):
        peers += [place(z_=up(z, step)), chip_at(step), chip_at(-step)]
        peers += [place(y_=up(y, step)), place(y_=up(y, step), core_=other)]
    for peer in peers:
        pl.semaphore_signal(barrier, inc=1, device_id=peer, device_id_type=MESH)

    loads = [
        pltpu.make_async_copy(src, dst, load_s.at[n])
        for n, (src, dst) in enumerate(
            [(q_hbm, q_in), (wk_hbm, wk), (og_hbm, og_in), (wv_hbm, wv), (qr_hbm, q_rope)]
        )
    ]
    for copy in loads:
        copy.start()

    def remote(src, dst, send, recv, peer):
        return pltpu.make_async_remote_copy(
            src_ref=src,
            dst_ref=dst,
            send_sem=send,
            recv_sem=recv,
            device_id=peer,
            device_id_type=MESH,
        )

    rope = rope_t[...].T
    rope = jnp.concatenate([rope, rope], axis=1)
    for quarter in range(4):
        rows = slice(quarter * 32, quarter * 32 + 32)
        kall[3, core, quarter, :, :LATENT] = latent[rows, :]
        kall[3, core, quarter, :, LATENT:] = rope[rows, :]
    pl.semaphore_wait(barrier, len(peers))

    own = remote(kall.at[3, core], kall.at[3, core], own_s, own_r, sibling)
    ahead = [
        remote(
            kall.at[3, core, y],
            kall.at[3 - step, core, y],
            ctx_s.at[step - 1],
            ctx_r.at[step - 1],
            chip_at(step),
        )
        for step in (1, 2, 3)
    ]
    for copy in ahead:
        copy.start()
    own.start()

    row, col = iota((NOPE, NOPE), 0), iota((NOPE, NOPE), 1)
    owner = ((row >> 4) & 3) * 32 + ((row >> 2) & 3) * 8 + (row >> 6) * 4 + (row & 3)
    by_owner = (col == owner).astype(F32).astype(BF16)
    eye = (col == row).astype(F32).astype(BF16)
    row, col = iota((64, 64), 0), iota((64, 64), 1)
    by_z = (col == ((row >> 2) & 3) * 16 + (row >> 4) * 4 + (row & 3)).astype(F32).astype(BF16)

    lane = iota((TOK, 2 * ROPE), 1)

    def project(head, carry):
        rows = pl.ds(pl.multiple_of(head * TOK, TOK), TOK)
        cols = pl.ds(pl.multiple_of(lax.div(head, 2) * 2 * ROPE, 2 * ROPE), 2 * ROPE)
        mine = gq_t[head]
        q_all[rows, :LATENT] = nn(mine, wk[head]).astype(BF16)
        keep = (lane < ROPE) == (lax.rem(head, 2) == 0)
        q_all[rows, LATENT:] = jnp.where(keep, q_rope[:, cols], jnp.zeros((), BF16))
        qt[head] = nt(by_owner, mine).astype(BF16)
        gt_all[:, rows] = nt(wv[head], og[head]).astype(BF16)
        return carry

    for copy in loads:
        copy.wait()
    gq_t[...] = jnp.swapaxes(q_in[...], 0, 1)
    og[...] = jnp.swapaxes(og_in[...], 0, 1)
    lax.fori_loop(0, HEADS // 2, project, 0)

    around = []
    for near in (1, 2, 3):
        ahead[near - 1].wait_recv()
        part = kall.at[3 - near, core, y]
        around.append(
            [
                remote(
                    part,
                    part,
                    yag_s.at[near - 1, step - 1],
                    yag_r.at[near - 1, step - 1],
                    place(y_=up(y, step)),
                )
                for step in (1, 2, 3)
            ]
        )
        for copy in around[-1]:
            copy.start()

    lax.fori_loop(HEADS // 2, HEADS, project, 0)

    query_pos = me * TOK + iota((1, TOK), 1)
    doc_start = jnp.zeros((1, TOK), jnp.int32)
    begin = jnp.int32(0)
    for doc in range(lengths.shape[0]):
        end = begin + lengths[doc]
        inside = (query_pos >= begin) & (query_pos < end)
        doc_start = doc_start + jnp.where(inside, begin, 0)
        begin = end
    for block in range(SPAN + 1):
        key_pos = (me - SPAN + block) * TOK + iota((TOK, TOK), 0)
        allowed = (key_pos >= doc_start) & (key_pos <= query_pos)
        bias[block * TOK : (block + 1) * TOK, :] = jnp.where(allowed, 0.0, -jnp.inf).astype(F32)

    across = []
    for near in (1, 2, 3):
        for copy in around[near - 1]:
            copy.wait_recv()
        part = kall.at[3 - near, core]
        across.append(remote(part, part, sib_s.at[near - 1], sib_r.at[near - 1], sibling))
        across[-1].start()
    own.wait_recv()
    for copy in across:
        copy.wait_recv()

    for block in range(SPAN + 1):
        at = core + block
        keys = kall[lax.div(at, 2), lax.rem(at, 2)].reshape(TOK, WIDE)
        kw[block * TOK : (block + 1) * TOK, :] = keys
        kwt[:, block * TOK : (block + 1) * TOK] = keys.T

    def w_stage0(g):
        return remote(w_out.at[g, other], w_r0.at[g], w0_s.at[g], w0_r.at[g], sibling)

    def w_stage1(g):
        return (
            remote(
                w_out.at[g, core, x_far, pl.ds(0, 32)],
                w_r1.at[g, 0],
                w1_s.at[g, 0],
                w1_r.at[g, 0],
                place(x_=x_next),
            ),
            remote(
                w_out.at[g, core, x_far, pl.ds(32, 32)],
                w_r1.at[g, 1],
                w1_s.at[g, 1],
                w1_r.at[g, 1],
                place(x_=x_prev),
            ),
        )

    def w_stage2(g):
        return (
            remote(
                w_out.at[g, core, x_next],
                w_r2.at[g, 0],
                w2_s.at[g, 0],
                w2_r.at[g, 0],
                place(x_=x_next),
            ),
            remote(
                w_out.at[g, core, x_prev],
                w_r2.at[g, 1],
                w2_s.at[g, 1],
                w2_r.at[g, 1],
                place(x_=x_prev),
            ),
        )

    def w_stage3(g):
        return [
            remote(
                w_v.at[g, up(z, step)],
                w_rz.at[g, step - 1],
                wz_s.at[g, step - 1],
                wz_r.at[g, step - 1],
                place(z_=up(z, step)),
            )
            for step in (1, 2, 3)
        ]

    def w_do1(g):
        w_stage0(g).wait_recv()

        def one(part, carry):
            w_out[g, core, part] = add(w_out[g, core, part], w_r0[g, part]).astype(BF16)
            return carry

        lax.fori_loop(0, 4, one, 0)
        for copy in w_stage1(g):
            copy.start()

    def w_do2(g):
        first, second = w_stage1(g)
        first.wait_recv()
        low = w_out[g, core, x_next, 0:32, :]
        w_out[g, core, x_next, 0:32, :] = add(low, w_r1[g, 0]).astype(BF16)
        second.wait_recv()
        high = w_out[g, core, x_prev, 32:64, :]
        w_out[g, core, x_prev, 32:64, :] = add(high, w_r1[g, 1]).astype(BF16)
        for copy in w_stage2(g):
            copy.start()

    def w_do3(g, of_key):
        for copy in w_stage2(g):
            copy.wait_recv()
        total = add(w_out[g, core, x], w_r2[g, 0], w_r2[g, 1]).astype(BF16)
        if of_key:
            total = nn(by_z, total).astype(BF16)
            for part in range(4):
                w_v[g, part] = total[part * 16 : part * 16 + 16, :]
        else:
            for part in range(4):
                for head in range(PACK):
                    w_v[g, part, :, head * 128 : head * 128 + 128] = total[
                        head * 16 : head * 16 + 16, part * 128 : part * 128 + 128
                    ]
        for copy in w_stage3(g):
            copy.start()

    def w_do4(g, of_key):
        for copy in w_stage3(g):
            copy.wait_recv()
        total = add(w_v[g, z], w_rz[g, 0], w_rz[g, 1], w_rz[g, 2]).astype(BF16)
        for local in range(PACK):
            if of_key:
                g_wk[(g - GROUPS) * PACK + local] = total[local * 4 : local * 4 + 4, :]
            else:
                g_wv[g * PACK + local] = total[:, local * 128 : local * 128 + 128]

    def group(g, carry):
        cols = pl.ds(pl.multiple_of(g * COLS, COLS), COLS)
        s_buf[...] = nt(kw[...], q_all[cols, :])
        @pl.when(g > 1)
        def _():
            w_do2(g - 2)

        @pl.when(g > 2)
        def _():
            w_do3(g - 3, False)

        high = jnp.full((1, COLS), -jnp.inf, F32)
        for block in range(SPAN + 1):
            rows = slice(block * TOK, (block + 1) * TOK)
            part = s_buf[rows, :] * SCALE + jnp.concatenate([bias[rows, :]] * PACK, axis=1)
            s_buf[rows, :] = part
            high = jnp.maximum(high, jnp.max(part, axis=0, keepdims=True))
        total = jnp.zeros((1, COLS), F32)
        for block in range(SPAN + 1):
            rows = slice(block * TOK, (block + 1) * TOK)
            part = jnp.exp(s_buf[rows, :] - high)
            s_buf[rows, :] = part
            total = total + jnp.sum(part, axis=0, keepdims=True)
        share = 1.0 / total
        for block in range(SPAN + 1):
            rows = slice(block * TOK, (block + 1) * TOK)
            part = s_buf[rows, :] * share
            s_buf[rows, :] = part
            p_all[rows, cols] = part.astype(BF16)

        @pl.when(g > 0)
        def _():
            w_do1(g - 1)

        gp_buf[...] = nn(kw[:, :LATENT], gt_all[:, cols])
        out_t = nn(kwt[:LATENT, :], p_all[:, cols]).astype(BF16)
        correction = jnp.sum(out_t.astype(F32) * gt_all[:, cols].astype(F32), axis=0, keepdims=True)
        for block in range(SPAN + 1):
            rows = slice(block * TOK, (block + 1) * TOK)
            part = SCALE * s_buf[rows, :] * (gp_buf[rows, :] - correction)
            ds_all[rows, cols] = part.astype(BF16)

        for local in range(PACK):
            gwv = nn(out_t[:, local * TOK : (local + 1) * TOK], og[g * PACK + local]).astype(BF16)
            rows = slice(local * 16, local * 16 + 16)
            for half in range(2):
                for part in range(4):
                    for depth in range(4):
                        begin = ((part * 4 + depth) * 2 + half) * 16
                        w_out[g, half, part, rows, depth * 128 : depth * 128 + 128] = gwv[
                            begin : begin + 16, :
                        ]
        w_stage0(g).start()

        return carry

    def second(g):
        cols = slice(g * COLS, (g + 1) * COLS)
        dq_t = nn(kwt[...], ds_all[:, cols]).astype(BF16)
        for local in range(PACK):
            head = g * PACK + local
            here = slice(local * TOK, (local + 1) * TOK)
            mine = dq_t[:LATENT, here]
            gq_t[head] = nt(eye, nn(wk[head], mine).astype(BF16)).astype(BF16)
            gwk = nt(qt[head], mine).astype(BF16)
            rows = slice(local * 16, local * 16 + 16)
            for half in range(2):
                for part in range(4):
                    begin = half * 64 + part * 16
                    w_out[GROUPS + g, half, part, rows, :] = gwk[begin : begin + 16, :]
        for pair in range(PACK // 2):
            left = dq_t[LATENT : LATENT + ROPE, pair * 256 : pair * 256 + 128]
            right = dq_t[LATENT + ROPE :, pair * 256 + 128 : pair * 256 + 256]
            both = nt(eye, jnp.concatenate([left, right], axis=0)).astype(BF16)
            gq_rope[:, (g * 2 + pair) * 128 : (g * 2 + pair + 1) * 128] = both
        w_stage0(GROUPS + g).start()

    lax.fori_loop(0, GROUPS, group, 0)
    last = GROUPS - 1

    def key_terms(first, after):
        rows = slice(first * TOK, after * TOK)
        wide = nn(ds_all[rows, :], q_all[...])
        narrow = wide[:, :LATENT] + nt(p_all[rows, :], gt_all[...])
        narrow, side = narrow.astype(BF16), wide[:, LATENT:].astype(BF16)
        for block in range(first, after):
            for quarter in range(4):
                for half in range(2):
                    begin = (block - first) * TOK + quarter * 32 + half * 16
                    kg[half, quarter, core + block, :, :LATENT] = narrow[begin : begin + 16, :]
                    kg[half, quarter, core + block, :, LATENT:] = side[begin : begin + 16, :]

    def e0(n):
        blocks = pl.ds(4 * n, 4)
        return remote(
            kg.at[other, :, blocks], k_r0.at[:, blocks], e0_s.at[n], e0_r.at[n], sibling
        )

    def e1(n):
        return [
            remote(
                kg.at[core, y_far, pl.ds(4 * n + 2 * way, 2)],
                k_r1.at[n, way],
                e1_s.at[n, way],
                e1_r.at[n, way],
                place(y_=y_to),
            )
            for way, y_to in ((0, y_next), (1, y_prev))
        ]

    def e2(n):
        return [
            remote(
                kg.at[core, y_to, pl.ds(4 * n, 4)],
                k_r2.at[n, way],
                e2_s.at[n, way],
                e2_r.at[n, way],
                place(y_=y_to),
            )
            for way, y_to in ((0, y_next), (1, y_prev))
        ]

    def e3(step):
        return remote(
            k_sum.at[pl.ds((3 - step) * 2, 2)],
            k_r3.at[step - 1],
            e3_s.at[step - 1],
            e3_r.at[step - 1],
            chip_at(-step),
        )

    def k_do1(n):
        e0(n).wait_recv()
        blocks = slice(4 * n, 4 * n + 4)
        for quarter in range(4):
            kg[core, quarter, blocks] = add(kg[core, quarter, blocks], k_r0[quarter, blocks]).astype(
                BF16
            )
        for copy in e1(n):
            copy.start()

    def k_do2(n):
        for way, (copy, y_to) in enumerate(zip(e1(n), (y_next, y_prev))):
            copy.wait_recv()
            blocks = slice(4 * n + 2 * way, 4 * n + 2 * way + 2)
            kg[core, y_to, blocks] = add(kg[core, y_to, blocks], k_r1[n, way]).astype(BF16)
        for copy in e2(n):
            copy.start()

    def k_do3(n):
        for copy in e2(n):
            copy.wait_recv()
        blocks = slice(4 * n, 4 * n + 4)
        k_sum[blocks] = add(kg[core, y, blocks], k_r2[n, 0], k_r2[n, 1]).astype(BF16)
        for step in ((3, 2), (1,))[n]:
            e3(step).start()

    for half in range(2):
        for quarter in range(4):
            kg[half, quarter, 7 * other] = jnp.zeros((16, WIDE), BF16)
    w_do2(last - 1)
    w_do3(last - 2, False)
    key_terms(0, 4)
    e0(0).start()
    w_do1(last)
    w_do3(last - 1, False)
    key_terms(4, 7)
    e0(1).start()
    w_do2(last)
    k_do1(0)
    second(0)
    k_do1(1)
    k_do2(0)
    w_do3(last, False)
    second(1)
    w_do1(GROUPS)
    k_do2(1)
    second(2)
    w_do1(GROUPS + 1)
    k_do3(0)
    w_do2(GROUPS)
    second(3)
    k_do3(1)
    w_do1(GROUPS + 2)
    w_do2(GROUPS + 1)
    w_do3(GROUPS, True)
    gq[...] = jnp.swapaxes(gq_t[...], 0, 1)
    w_do1(GROUPS + 3)
    w_do2(GROUPS + 2)
    for step in (1, 2, 3):
        e3(step).wait_recv()
    k_mid[...] = add(k_sum[6:8], k_r3[0], k_r3[1], k_r3[2]).astype(BF16)
    e4 = remote(k_mid, k_r4, e4_s, e4_r, place(zh_=1 - zh))
    e4.start()
    w_do3(GROUPS + 1, True)
    w_do2(GROUPS + 3)
    w_do3(GROUPS + 2, True)
    e4.wait_recv()
    total = add(k_mid[...], k_r4[...])
    k_fin[:, :, :LATENT] = total[:, :, :LATENT].astype(BF16)
    rope_part = total[:, :, LATENT:].reshape(32, 2 * ROPE)
    rope_part = rope_part + pltpu.roll(rope_part, ROPE, 1)
    k_fin[:, :, LATENT:] = rope_part.reshape(2, 16, 2 * ROPE).astype(BF16)
    k_out[y, core] = k_fin[core]
    e5 = [
        remote(
            k_fin.at[core],
            k_out.at[y, core],
            e5_s.at[step - 1],
            e5_r.at[step - 1],
            place(y_=up(y, step)),
        )
        for step in (1, 2, 3)
    ] + [
        remote(
            k_fin.at[other],
            k_out.at[y, core],
            e5_s.at[3 + step],
            e5_r.at[3 + step],
            place(y_=up(y, step), core_=other),
        )
        for step in (0, 1, 2, 3)
    ]
    for copy in e5:
        copy.start()
    for g in range(GROUPS):
        w_do4(g, False)
    w_do3(GROUPS + 3, True)
    for copy in e5:
        copy.wait_recv()
    for quarter in range(4):
        for half in range(2):
            begin = quarter * 32 + half * 16
            g_latent[begin : begin + 16, :] = k_out[quarter, half, :, :LATENT]
    g_rope_t[...] = k_out[:, :, :, LATENT:].reshape(TOK, 2 * ROPE).T[:ROPE, :]
    for g in range(GROUPS, JOBS):
        w_do4(g, True)

    own.wait_send()
    e4.wait_send()
    for n in range(2):
        for copy in [e0(n), *e1(n), *e2(n)]:
            copy.wait_send()
    for copy in [*ahead, *across, *e5, *(copy for three in around for copy in three)]:
        copy.wait_send()
    for step in (1, 2, 3):
        e3(step).wait_send()
    for g in range(JOBS):
        for copy in [w_stage0(g), *w_stage1(g), *w_stage2(g), *w_stage3(g)]:
            copy.wait_send()


def hand_over(*refs):
    count = len(refs) // 2
    for source, target in zip(refs[:count], refs[count:]):
        target[...] = source[...]


def per_device(q_nope, q_rope, latent, k_rope, out_grad, w_key, w_value, lengths):
    dma = pltpu.SemaphoreType.DMA
    vmem = pl.BlockSpec(memory_space=pltpu.VMEM)
    hbm = pl.BlockSpec(memory_space=pl.ANY)

    def held(*shape, dtype=BF16):
        return pltpu.VMEM(shape, dtype)

    out = pl.pallas_call(
        kernel,
        out_shape=(
            jax.ShapeDtypeStruct((TOK, HEADS, NOPE), BF16),
            jax.ShapeDtypeStruct((TOK, HEADS * ROPE), BF16),
            jax.ShapeDtypeStruct((TOK, LATENT), BF16),
            jax.ShapeDtypeStruct((ROPE, TOK), BF16),
            jax.ShapeDtypeStruct((HEADS, 4, LATENT), BF16),
            jax.ShapeDtypeStruct((HEADS, 16, NOPE), BF16),
        ),
        in_specs=[pl.BlockSpec(memory_space=pltpu.SMEM), hbm, hbm, vmem, vmem, hbm, hbm, hbm],
        out_specs=[vmem] * 6,
        scratch_shapes=[
            held(TOK, HEADS, NOPE),
            held(TOK, HEADS, NOPE),
            held(TOK, HEADS * ROPE),
            held(HEADS, NOPE, LATENT),
            held(HEADS, LATENT, NOPE),
            held(HEADS, TOK, NOPE),
            held(HEADS, NOPE, TOK),
            held(HEADS, TOK, NOPE),
            held(4, 2, 4, 32, WIDE),
            held(WINDOW, WIDE),
            held(WIDE, WINDOW),
            held(HEADS * TOK, WIDE),
            held(LATENT, HEADS * TOK),
            held(WINDOW, HEADS * TOK),
            held(WINDOW, HEADS * TOK),
            held(WINDOW, COLS, dtype=F32),
            held(WINDOW, COLS, dtype=F32),
            held(WINDOW, TOK, dtype=F32),
            held(JOBS, 2, 4, 64, LATENT),
            held(JOBS, 4, 64, LATENT),
            held(JOBS, 2, 32, LATENT),
            held(JOBS, 2, 64, LATENT),
            held(JOBS, 4, 16, LATENT),
            held(JOBS, 3, 16, LATENT),
            held(2, 4, 8, 16, WIDE),
            held(4, 8, 16, WIDE),
            held(2, 2, 2, 16, WIDE),
            held(2, 2, 4, 16, WIDE),
            held(8, 16, WIDE),
            held(3, 2, 16, WIDE),
            held(2, 16, WIDE),
            held(2, 16, WIDE),
            held(2, 16, WIDE),
            held(4, 2, 16, WIDE),
            dma((5,)),
            dma,
            dma,
            dma((3,)),
            dma((3,)),
            dma((3, 3)),
            dma((3, 3)),
            dma((3,)),
            dma((3,)),
            dma((JOBS,)),
            dma((JOBS,)),
            dma((JOBS, 2)),
            dma((JOBS, 2)),
            dma((JOBS, 2)),
            dma((JOBS, 2)),
            dma((JOBS, 3)),
            dma((JOBS, 3)),
            dma((2,)),
            dma((2,)),
            dma((2, 2)),
            dma((2, 2)),
            dma((2, 2)),
            dma((2, 2)),
            dma((3,)),
            dma((3,)),
            dma,
            dma,
            dma((7,)),
            dma((7,)),
        ],
        compiler_params=pltpu.CompilerParams(
            collective_id=0, has_side_effects=True, vmem_limit_bytes=58 * 2**20
        ),
        cost_estimate=pl.CostEstimate(
            flops=15 * 10**9, bytes_accessed=8 * 10**6, transcendentals=2 * 10**6
        ),
        name="mla_backward",
    )(
        lengths,
        q_nope,
        q_rope,
        latent,
        k_rope.T,
        out_grad,
        w_key,
        w_value,
    )
    gq, gq_rope, g_latent, g_rope_t, g_wk, g_wv = pl.pallas_call(
        hand_over,
        out_shape=tuple(jax.ShapeDtypeStruct(array.shape, array.dtype) for array in out),
        in_specs=[vmem] * len(out),
        out_specs=[vmem] * len(out),
        name="hand_over",
    )(*out)
    return gq, gq_rope, g_latent, g_rope_t.T, g_wk, g_wv


def solution(mesh):
    placed = (
        P("ctx", "tp", None),
        P("ctx", "tp"),
        P("ctx", None),
        P("ctx", None),
        P("ctx", "tp", None),
        P("tp", None, None),
        P("tp", None, None),
        P(),
    )
    return jax.shard_map(
        per_device,
        mesh=mesh,
        in_specs=placed,
        out_specs=(
            P("ctx", "tp", None),
            P("ctx", "tp"),
            P("ctx", None),
            P("ctx", None),
            P("tp", "ctx", None),
            P("tp", "ctx", None),
        ),
        check_vma=False,
    )
```

```python
import jax
import jax.numpy as jnp
from jax import lax
from jax.experimental import pallas as pl
from jax.experimental.pallas import tpu as pltpu
from jax.sharding import PartitionSpec as P

NOPE = 128
ROPE = 64
LATENT = 512
WIDE = LATENT + 2 * ROPE
TOK = 128
SPAN = 6
WINDOW = (SPAN + 1) * TOK
HEADS = 16
PACK = 4
GROUPS = HEADS // PACK
JOBS = 2 * GROUPS
COLS = PACK * TOK
SCALE = float(NOPE + ROPE) ** -0.5
MESH = pl.DeviceIdType.MESH
F32 = jnp.float32
BF16 = jnp.bfloat16


def nn(a, b):
    return lax.dot_general(a, b, (((1,), (0,)), ((), ())), preferred_element_type=F32)


def nt(a, b):
    return lax.dot_general(a, b, (((1,), (1,)), ((), ())), preferred_element_type=F32)


def add(*terms):
    total = terms[0].astype(F32)
    for term in terms[1:]:
        total = total + term.astype(F32)
    return total


def iota(shape, dim):
    return lax.broadcasted_iota(jnp.int32, shape, dim)


def kernel(
    lengths,
    q_hbm,
    qr_hbm,
    latent,
    rope_t,
    og_hbm,
    wk_hbm,
    wv_hbm,
    gq,
    gq_rope,
    g_latent,
    g_rope_t,
    g_wk,
    g_wv,
    q_in,
    og_in,
    q_rope,
    wk,
    wv,
    og,
    qt,
    gq_t,
    kall,
    kw,
    kwt,
    q_all,
    gt_all,
    p_all,
    ds_all,
    s_buf,
    gp_buf,
    bias,
    w_out,
    w_r0,
    w_r1,
    w_v,
    w_rz,
    kg,
    k_r0,
    k_r1,
    k_sum,
    k_r3,
    k_mid,
    k_r4,
    k_fin,
    k_out,
    load_s,
    own_s,
    own_r,
    ctx_s,
    ctx_r,
    yag_s,
    yag_r,
    sib_s,
    sib_r,
    w0_s,
    w0_r,
    w1_s,
    w1_r,
    wz_s,
    wz_r,
    e0_s,
    e0_r,
    e1_s,
    e1_r,
    e3_s,
    e3_r,
    e4_s,
    e4_r,
    e5_s,
    e5_r,
):
    me = lax.axis_index("ctx")
    tp = lax.axis_index("tp")
    core = lax.rem(me, 2)
    chip = lax.div(me, 2)
    z = lax.rem(chip, 4)
    x = lax.div(chip, 4)
    y = lax.rem(tp, 4)
    zh = lax.div(tp, 4)
    other = 1 - core

    def place(x_=x, z_=z, core_=core, y_=y, zh_=zh):
        return ((x_ * 4 + z_) * 2 + core_, zh_ * 4 + y_)

    def up(value, step):
        return lax.rem(value + step, 4)

    def chip_at(step):
        return (lax.rem(chip + step + 16, 16) * 2 + core, tp)

    sibling = place(core_=other)

    barrier = pltpu.get_barrier_semaphore()
    peers = [sibling, place(zh_=1 - zh)]
    for step in (1, 2, 3):
        peers += [place(x_=up(x, step)), place(z_=up(z, step)), chip_at(step), chip_at(-step)]
        peers += [place(y_=up(y, step)), place(y_=up(y, step), core_=other)]
    for peer in peers:
        pl.semaphore_signal(barrier, inc=1, device_id=peer, device_id_type=MESH)

    loads = [
        pltpu.make_async_copy(src, dst, load_s.at[n])
        for n, (src, dst) in enumerate(
            [(q_hbm, q_in), (wk_hbm, wk), (og_hbm, og_in), (wv_hbm, wv), (qr_hbm, q_rope)]
        )
    ]
    for copy in loads:
        copy.start()

    def remote(src, dst, send, recv, peer):
        return pltpu.make_async_remote_copy(
            src_ref=src,
            dst_ref=dst,
            send_sem=send,
            recv_sem=recv,
            device_id=peer,
            device_id_type=MESH,
        )

    rope = rope_t[...].T
    rope = jnp.concatenate([rope, rope], axis=1)
    for quarter in range(4):
        rows = slice(quarter * 32, quarter * 32 + 32)
        kall[3, core, quarter, :, :LATENT] = latent[rows, :]
        kall[3, core, quarter, :, LATENT:] = rope[rows, :]
    pl.semaphore_wait(barrier, len(peers))

    own = remote(kall.at[3, core], kall.at[3, core], own_s, own_r, sibling)
    ahead = [
        remote(
            kall.at[3, core, y],
            kall.at[3 - step, core, y],
            ctx_s.at[step - 1],
            ctx_r.at[step - 1],
            chip_at(step),
        )
        for step in (1, 2, 3)
    ]
    for copy in ahead:
        copy.start()
    own.start()

    row, col = iota((NOPE, NOPE), 0), iota((NOPE, NOPE), 1)
    owner = ((row >> 4) & 3) * 32 + ((row >> 2) & 3) * 8 + (row >> 6) * 4 + (row & 3)
    by_owner = (col == owner).astype(F32).astype(BF16)
    eye = (col == row).astype(F32).astype(BF16)
    row, col = iota((64, 64), 0), iota((64, 64), 1)
    by_z = (col == ((row >> 2) & 3) * 16 + (row >> 4) * 4 + (row & 3)).astype(F32).astype(BF16)

    lane = iota((TOK, 2 * ROPE), 1)

    def project(head, carry):
        rows = pl.ds(pl.multiple_of(head * TOK, TOK), TOK)
        cols = pl.ds(pl.multiple_of(lax.div(head, 2) * 2 * ROPE, 2 * ROPE), 2 * ROPE)
        mine = gq_t[head]
        q_all[rows, :LATENT] = nn(mine, wk[head]).astype(BF16)
        keep = (lane < ROPE) == (lax.rem(head, 2) == 0)
        q_all[rows, LATENT:] = jnp.where(keep, q_rope[:, cols], jnp.zeros((), BF16))
        qt[head] = nt(by_owner, mine).astype(BF16)
        gt_all[:, rows] = nt(wv[head], og[head]).astype(BF16)
        return carry

    for copy in loads:
        copy.wait()
    gq_t[...] = jnp.swapaxes(q_in[...], 0, 1)
    og[...] = jnp.swapaxes(og_in[...], 0, 1)
    lax.fori_loop(0, HEADS // 2, project, 0)

    around = []
    for near in (1, 2, 3):
        ahead[near - 1].wait_recv()
        part = kall.at[3 - near, core, y]
        around.append(
            [
                remote(
                    part,
                    part,
                    yag_s.at[near - 1, step - 1],
                    yag_r.at[near - 1, step - 1],
                    place(y_=up(y, step)),
                )
                for step in (1, 2, 3)
            ]
        )
        for copy in around[-1]:
            copy.start()

    lax.fori_loop(HEADS // 2, HEADS, project, 0)

    query_pos = me * TOK + iota((1, TOK), 1)
    doc_start = jnp.zeros((1, TOK), jnp.int32)
    begin = jnp.int32(0)
    for doc in range(lengths.shape[0]):
        end = begin + lengths[doc]
        inside = (query_pos >= begin) & (query_pos < end)
        doc_start = doc_start + jnp.where(inside, begin, 0)
        begin = end
    for block in range(SPAN + 1):
        key_pos = (me - SPAN + block) * TOK + iota((TOK, TOK), 0)
        allowed = (key_pos >= doc_start) & (key_pos <= query_pos)
        bias[block * TOK : (block + 1) * TOK, :] = jnp.where(allowed, 0.0, -jnp.inf).astype(F32)

    across = []
    for near in (1, 2, 3):
        for copy in around[near - 1]:
            copy.wait_recv()
        part = kall.at[3 - near, core]
        across.append(remote(part, part, sib_s.at[near - 1], sib_r.at[near - 1], sibling))
        across[-1].start()
    own.wait_recv()
    for copy in across:
        copy.wait_recv()

    for block in range(SPAN + 1):
        at = core + block
        keys = kall[lax.div(at, 2), lax.rem(at, 2)].reshape(TOK, WIDE)
        kw[block * TOK : (block + 1) * TOK, :] = keys
        kwt[:, block * TOK : (block + 1) * TOK] = keys.T

    def w_stage0(g):
        return remote(w_out.at[g, other], w_r0.at[g], w0_s.at[g], w0_r.at[g], sibling)

    def w_stage1(g):
        return [
            remote(
                w_out.at[g, core, up(x, step)],
                w_r1.at[g, step - 1],
                w1_s.at[g, step - 1],
                w1_r.at[g, step - 1],
                place(x_=up(x, step)),
            )
            for step in (2, 1, 3)
        ]

    def w_stage2(g):
        return [
            remote(
                w_v.at[g, up(z, step)],
                w_rz.at[g, step - 1],
                wz_s.at[g, step - 1],
                wz_r.at[g, step - 1],
                place(z_=up(z, step)),
            )
            for step in (1, 2, 3)
        ]

    def w_do1(g):
        w_stage0(g).wait_recv()

        def one(part, carry):
            w_out[g, core, part] = add(w_out[g, core, part], w_r0[g, part]).astype(BF16)
            return carry

        lax.fori_loop(0, 4, one, 0)
        for copy in w_stage1(g):
            copy.start()

    def w_do2(g, of_key):
        for copy in w_stage1(g):
            copy.wait_recv()
        total = add(w_out[g, core, x], w_r1[g, 0], w_r1[g, 1], w_r1[g, 2]).astype(BF16)
        if of_key:
            total = nn(by_z, total).astype(BF16)
            for part in range(4):
                w_v[g, part] = total[part * 16 : part * 16 + 16, :]
        else:
            for part in range(4):
                for head in range(PACK):
                    w_v[g, part, :, head * 128 : head * 128 + 128] = total[
                        head * 16 : head * 16 + 16, part * 128 : part * 128 + 128
                    ]
        for copy in w_stage2(g):
            copy.start()

    def w_do3(g, of_key):
        for copy in w_stage2(g):
            copy.wait_recv()
        total = add(w_v[g, z], w_rz[g, 0], w_rz[g, 1], w_rz[g, 2]).astype(BF16)
        for local in range(PACK):
            if of_key:
                g_wk[(g - GROUPS) * PACK + local] = total[local * 4 : local * 4 + 4, :]
            else:
                g_wv[g * PACK + local] = total[:, local * 128 : local * 128 + 128]

    def group(g, carry):
        cols = pl.ds(pl.multiple_of(g * COLS, COLS), COLS)
        s_buf[...] = nt(kw[...], q_all[cols, :])
        high = jnp.full((1, COLS), -jnp.inf, F32)
        for block in range(SPAN + 1):
            rows = slice(block * TOK, (block + 1) * TOK)
            part = s_buf[rows, :] * SCALE + jnp.concatenate([bias[rows, :]] * PACK, axis=1)
            s_buf[rows, :] = part
            high = jnp.maximum(high, jnp.max(part, axis=0, keepdims=True))
        total = jnp.zeros((1, COLS), F32)
        for block in range(SPAN + 1):
            rows = slice(block * TOK, (block + 1) * TOK)
            part = jnp.exp(s_buf[rows, :] - high)
            s_buf[rows, :] = part
            total = total + jnp.sum(part, axis=0, keepdims=True)
        share = 1.0 / total
        for block in range(SPAN + 1):
            rows = slice(block * TOK, (block + 1) * TOK)
            part = s_buf[rows, :] * share
            s_buf[rows, :] = part
            p_all[rows, cols] = part.astype(BF16)

        @pl.when(g > 0)
        def _():
            w_do1(g - 1)

        gp_buf[...] = nn(kw[:, :LATENT], gt_all[:, cols])
        out_t = nn(kwt[:LATENT, :], p_all[:, cols]).astype(BF16)
        correction = jnp.sum(out_t.astype(F32) * gt_all[:, cols].astype(F32), axis=0, keepdims=True)
        for block in range(SPAN + 1):
            rows = slice(block * TOK, (block + 1) * TOK)
            part = SCALE * s_buf[rows, :] * (gp_buf[rows, :] - correction)
            ds_all[rows, cols] = part.astype(BF16)

        for local in range(PACK):
            gwv = nn(out_t[:, local * TOK : (local + 1) * TOK], og[g * PACK + local]).astype(BF16)
            rows = slice(local * 16, local * 16 + 16)
            for half in range(2):
                for part in range(4):
                    for depth in range(4):
                        begin = ((part * 4 + depth) * 2 + half) * 16
                        w_out[g, half, part, rows, depth * 128 : depth * 128 + 128] = gwv[
                            begin : begin + 16, :
                        ]
        w_stage0(g).start()

        @pl.when(g > 1)
        def _():
            w_do2(g - 2, False)

        return carry

    def second(g):
        cols = slice(g * COLS, (g + 1) * COLS)
        dq_t = nn(kwt[...], ds_all[:, cols]).astype(BF16)
        for local in range(PACK):
            head = g * PACK + local
            here = slice(local * TOK, (local + 1) * TOK)
            mine = dq_t[:LATENT, here]
            gq_t[head] = nt(eye, nn(wk[head], mine).astype(BF16)).astype(BF16)
            gwk = nt(qt[head], mine).astype(BF16)
            rows = slice(local * 16, local * 16 + 16)
            for half in range(2):
                for part in range(4):
                    begin = half * 64 + part * 16
                    w_out[GROUPS + g, half, part, rows, :] = gwk[begin : begin + 16, :]
        for pair in range(PACK // 2):
            left = dq_t[LATENT : LATENT + ROPE, pair * 256 : pair * 256 + 128]
            right = dq_t[LATENT + ROPE :, pair * 256 + 128 : pair * 256 + 256]
            both = nt(eye, jnp.concatenate([left, right], axis=0)).astype(BF16)
            gq_rope[:, (g * 2 + pair) * 128 : (g * 2 + pair + 1) * 128] = both
        w_stage0(GROUPS + g).start()

    lax.fori_loop(0, GROUPS, group, 0)
    last = GROUPS - 1

    def key_terms(first, after, between):
        rows = slice(first * TOK, after * TOK)
        wide = nn(ds_all[rows, :], q_all[...])
        between()
        narrow = wide[:, :LATENT] + nt(p_all[rows, :], gt_all[...])
        narrow, side = narrow.astype(BF16), wide[:, LATENT:].astype(BF16)
        for block in range(first, after):
            for quarter in range(4):
                for half in range(2):
                    begin = (block - first) * TOK + quarter * 32 + half * 16
                    kg[half, quarter, core + block, :, :LATENT] = narrow[begin : begin + 16, :]
                    kg[half, quarter, core + block, :, LATENT:] = side[begin : begin + 16, :]

    def e0(n):
        blocks = pl.ds(4 * n, 4)
        return remote(
            kg.at[other, :, blocks], k_r0.at[:, blocks], e0_s.at[n], e0_r.at[n], sibling
        )

    def e1(n):
        blocks = pl.ds(4 * n, 4)
        return [
            remote(
                kg.at[core, up(y, step), blocks],
                k_r1.at[n, step - 1],
                e1_s.at[n, step - 1],
                e1_r.at[n, step - 1],
                place(y_=up(y, step)),
            )
            for step in (2, 1, 3)
        ]

    def e3(step):
        return remote(
            k_sum.at[pl.ds((3 - step) * 2, 2)],
            k_r3.at[step - 1],
            e3_s.at[step - 1],
            e3_r.at[step - 1],
            chip_at(-step),
        )

    def k_do1(n):
        e0(n).wait_recv()
        blocks = slice(4 * n, 4 * n + 4)
        for quarter in range(4):
            kg[core, quarter, blocks] = add(kg[core, quarter, blocks], k_r0[quarter, blocks]).astype(
                BF16
            )
        for copy in e1(n):
            copy.start()

    def k_do2(n):
        for copy in e1(n):
            copy.wait_recv()
        blocks = slice(4 * n, 4 * n + 4)
        k_sum[blocks] = add(kg[core, y, blocks], k_r1[n, 0], k_r1[n, 1], k_r1[n, 2]).astype(BF16)
        for step in ((3, 2), (1,))[n]:
            e3(step).start()

    for half in range(2):
        for quarter in range(4):
            kg[half, quarter, 7 * other] = jnp.zeros((16, WIDE), BF16)
    key_terms(0, 4, lambda: w_do1(last))
    e0(0).start()
    key_terms(4, 7, lambda: k_do1(0))
    e0(1).start()
    w_do2(last - 1, False)
    second(0)
    k_do1(1)
    second(1)
    w_do1(GROUPS)
    w_do2(last, False)
    second(2)
    k_do2(0)
    w_do1(GROUPS + 1)
    second(3)
    k_do2(1)
    w_do1(GROUPS + 2)
    gq[...] = jnp.swapaxes(gq_t[...], 0, 1)
    w_do1(GROUPS + 3)
    w_do2(GROUPS, True)
    for step in (1, 2, 3):
        e3(step).wait_recv()
    k_mid[...] = add(k_sum[6:8], k_r3[0], k_r3[1], k_r3[2]).astype(BF16)
    e4 = remote(k_mid, k_r4, e4_s, e4_r, place(zh_=1 - zh))
    e4.start()
    w_do2(GROUPS + 1, True)
    w_do2(GROUPS + 2, True)
    w_do2(GROUPS + 3, True)
    for g in range(GROUPS):
        w_do3(g, False)
    e4.wait_recv()
    total = add(k_mid[...], k_r4[...])
    k_fin[:, :, :LATENT] = total[:, :, :LATENT].astype(BF16)
    rope_part = total[:, :, LATENT:].reshape(32, 2 * ROPE)
    rope_part = rope_part + pltpu.roll(rope_part, ROPE, 1)
    k_fin[:, :, LATENT:] = rope_part.reshape(2, 16, 2 * ROPE).astype(BF16)
    k_out[y, core] = k_fin[core]
    e5 = [
        remote(
            k_fin.at[core],
            k_out.at[y, core],
            e5_s.at[step - 1],
            e5_r.at[step - 1],
            place(y_=up(y, step)),
        )
        for step in (1, 2, 3)
    ] + [
        remote(
            k_fin.at[other],
            k_out.at[y, core],
            e5_s.at[3 + step],
            e5_r.at[3 + step],
            place(y_=up(y, step), core_=other),
        )
        for step in (0, 1, 2, 3)
    ]
    for copy in e5:
        copy.start()
    for copy in e5:
        copy.wait_recv()
    for quarter in range(4):
        for half in range(2):
            begin = quarter * 32 + half * 16
            g_latent[begin : begin + 16, :] = k_out[quarter, half, :, :LATENT]
    g_rope_t[...] = k_out[:, :, :, LATENT:].reshape(TOK, 2 * ROPE).T[:ROPE, :]
    for g in range(GROUPS, JOBS):
        w_do3(g, True)

    own.wait_send()
    e4.wait_send()
    for n in range(2):
        for copy in [e0(n), *e1(n)]:
            copy.wait_send()
    for copy in [*ahead, *across, *e5, *(copy for three in around for copy in three)]:
        copy.wait_send()
    for step in (1, 2, 3):
        e3(step).wait_send()
    for g in range(JOBS):
        for copy in [w_stage0(g), *w_stage1(g), *w_stage2(g)]:
            copy.wait_send()


def hand_over(*refs):
    count = len(refs) // 2
    for source, target in zip(refs[:count], refs[count:]):
        target[...] = source[...]


def per_device(q_nope, q_rope, latent, k_rope, out_grad, w_key, w_value, lengths):
    dma = pltpu.SemaphoreType.DMA
    vmem = pl.BlockSpec(memory_space=pltpu.VMEM)
    hbm = pl.BlockSpec(memory_space=pl.ANY)

    def held(*shape, dtype=BF16):
        return pltpu.VMEM(shape, dtype)

    out = pl.pallas_call(
        kernel,
        out_shape=(
            jax.ShapeDtypeStruct((TOK, HEADS, NOPE), BF16),
            jax.ShapeDtypeStruct((TOK, HEADS * ROPE), BF16),
            jax.ShapeDtypeStruct((TOK, LATENT), BF16),
            jax.ShapeDtypeStruct((ROPE, TOK), BF16),
            jax.ShapeDtypeStruct((HEADS, 4, LATENT), BF16),
            jax.ShapeDtypeStruct((HEADS, 16, NOPE), BF16),
        ),
        in_specs=[pl.BlockSpec(memory_space=pltpu.SMEM), hbm, hbm, vmem, vmem, hbm, hbm, hbm],
        out_specs=[vmem] * 6,
        scratch_shapes=[
            held(TOK, HEADS, NOPE),
            held(TOK, HEADS, NOPE),
            held(TOK, HEADS * ROPE),
            held(HEADS, NOPE, LATENT),
            held(HEADS, LATENT, NOPE),
            held(HEADS, TOK, NOPE),
            held(HEADS, NOPE, TOK),
            held(HEADS, TOK, NOPE),
            held(4, 2, 4, 32, WIDE),
            held(WINDOW, WIDE),
            held(WIDE, WINDOW),
            held(HEADS * TOK, WIDE),
            held(LATENT, HEADS * TOK),
            held(WINDOW, HEADS * TOK),
            held(WINDOW, HEADS * TOK),
            held(WINDOW, COLS, dtype=F32),
            held(WINDOW, COLS, dtype=F32),
            held(WINDOW, TOK, dtype=F32),
            held(JOBS, 2, 4, 64, LATENT),
            held(JOBS, 4, 64, LATENT),
            held(JOBS, 3, 64, LATENT),
            held(JOBS, 4, 16, LATENT),
            held(JOBS, 3, 16, LATENT),
            held(2, 4, 8, 16, WIDE),
            held(4, 8, 16, WIDE),
            held(2, 3, 4, 16, WIDE),
            held(8, 16, WIDE),
            held(3, 2, 16, WIDE),
            held(2, 16, WIDE),
            held(2, 16, WIDE),
            held(2, 16, WIDE),
            held(4, 2, 16, WIDE),
            dma((5,)),
            dma,
            dma,
            dma((3,)),
            dma((3,)),
            dma((3, 3)),
            dma((3, 3)),
            dma((3,)),
            dma((3,)),
            dma((JOBS,)),
            dma((JOBS,)),
            dma((JOBS, 3)),
            dma((JOBS, 3)),
            dma((JOBS, 3)),
            dma((JOBS, 3)),
            dma((2,)),
            dma((2,)),
            dma((2, 3)),
            dma((2, 3)),
            dma((3,)),
            dma((3,)),
            dma,
            dma,
            dma((7,)),
            dma((7,)),
        ],
        compiler_params=pltpu.CompilerParams(
            collective_id=0, has_side_effects=True, vmem_limit_bytes=58 * 2**20
        ),
        cost_estimate=pl.CostEstimate(
            flops=15 * 10**9, bytes_accessed=8 * 10**6, transcendentals=2 * 10**6
        ),
        name="mla_backward",
    )(
        lengths,
        q_nope,
        q_rope,
        latent,
        k_rope.T,
        out_grad,
        w_key,
        w_value,
    )
    gq, gq_rope, g_latent, g_rope_t, g_wk, g_wv = pl.pallas_call(
        hand_over,
        out_shape=tuple(jax.ShapeDtypeStruct(array.shape, array.dtype) for array in out),
        in_specs=[vmem] * len(out),
        out_specs=[vmem] * len(out),
        name="hand_over",
    )(*out)
    return gq, gq_rope, g_latent, g_rope_t.T, g_wk, g_wv


def solution(mesh):
    placed = (
        P("ctx", "tp", None),
        P("ctx", "tp"),
        P("ctx", None),
        P("ctx", None),
        P("ctx", "tp", None),
        P("tp", None, None),
        P("tp", None, None),
        P(),
    )
    return jax.shard_map(
        per_device,
        mesh=mesh,
        in_specs=placed,
        out_specs=(
            P("ctx", "tp", None),
            P("ctx", "tp"),
            P("ctx", None),
            P("ctx", None),
            P("tp", "ctx", None),
            P("tp", "ctx", None),
        ),
        check_vma=False,
    )
```

```python
import jax
import jax.numpy as jnp
from jax import lax
from jax.experimental import pallas as pl
from jax.experimental.pallas import tpu as pltpu
from jax.sharding import PartitionSpec as P

NOPE = 128
ROPE = 64
LATENT = 512
WIDE = LATENT + 2 * ROPE
TOK = 128
SPAN = 6
WINDOW = (SPAN + 1) * TOK
HEADS = 16
PACK = 4
GROUPS = HEADS // PACK
JOBS = 2 * GROUPS
COLS = PACK * TOK
SCALE = float(NOPE + ROPE) ** -0.5
MESH = pl.DeviceIdType.MESH
F32 = jnp.float32
BF16 = jnp.bfloat16


def nn(a, b):
    return lax.dot_general(a, b, (((1,), (0,)), ((), ())), preferred_element_type=F32)


def nt(a, b):
    return lax.dot_general(a, b, (((1,), (1,)), ((), ())), preferred_element_type=F32)


def add(*terms):
    total = terms[0].astype(F32)
    for term in terms[1:]:
        total = total + term.astype(F32)
    return total


def iota(shape, dim):
    return lax.broadcasted_iota(jnp.int32, shape, dim)


def kernel(
    lengths,
    q_hbm,
    qr_hbm,
    latent,
    rope_t,
    og_hbm,
    wk_hbm,
    wv_hbm,
    gq,
    gq_rope,
    g_latent,
    g_rope_t,
    g_wk,
    g_wv,
    q_in,
    og_in,
    q_rope,
    wk,
    wv,
    og,
    qt,
    gq_t,
    gq_v,
    gqr_v,
    dq_all,
    kall,
    kw,
    kwt,
    q_all,
    gt_all,
    p_all,
    ds_all,
    s_buf,
    gp_buf,
    bias,
    w_out,
    w_r0,
    w_r1,
    w_v,
    w_rz,
    kg,
    k_r0,
    k_r1,
    k_sum,
    k_r3,
    k_mid,
    k_r4,
    k_fin,
    k_out,
    load_s,
    leave_s,
    own_s,
    own_r,
    ctx_s,
    ctx_r,
    yag_s,
    yag_r,
    sib_s,
    sib_r,
    w0_s,
    w0_r,
    w1_s,
    w1_r,
    wz_s,
    wz_r,
    e0_s,
    e0_r,
    e1_s,
    e1_r,
    e3_s,
    e3_r,
    e4_s,
    e4_r,
    e5_s,
    e5_r,
):
    me = lax.axis_index("ctx")
    tp = lax.axis_index("tp")
    core = lax.rem(me, 2)
    chip = lax.div(me, 2)
    z = lax.rem(chip, 4)
    x = lax.div(chip, 4)
    y = lax.rem(tp, 4)
    zh = lax.div(tp, 4)
    other = 1 - core

    def place(x_=x, z_=z, core_=core, y_=y, zh_=zh):
        return ((x_ * 4 + z_) * 2 + core_, zh_ * 4 + y_)

    def up(value, step):
        return lax.rem(value + step, 4)

    def chip_at(step):
        return (lax.rem(chip + step + 16, 16) * 2 + core, tp)

    sibling = place(core_=other)

    barrier = pltpu.get_barrier_semaphore()
    peers = [sibling, place(zh_=1 - zh)]
    for step in (1, 2, 3):
        peers += [place(x_=up(x, step)), place(z_=up(z, step)), chip_at(step), chip_at(-step)]
        peers += [place(y_=up(y, step)), place(y_=up(y, step), core_=other)]
    for peer in peers:
        pl.semaphore_signal(barrier, inc=1, device_id=peer, device_id_type=MESH)

    loads = [
        pltpu.make_async_copy(src, dst, load_s.at[n])
        for n, (src, dst) in enumerate(
            [(q_hbm, q_in), (wk_hbm, wk), (og_hbm, og_in), (wv_hbm, wv), (qr_hbm, q_rope)]
        )
    ]
    for copy in loads:
        copy.start()

    def remote(src, dst, send, recv, peer):
        return pltpu.make_async_remote_copy(
            src_ref=src,
            dst_ref=dst,
            send_sem=send,
            recv_sem=recv,
            device_id=peer,
            device_id_type=MESH,
        )

    rope = rope_t[...].T
    rope = jnp.concatenate([rope, rope], axis=1)
    for quarter in range(4):
        rows = slice(quarter * 32, quarter * 32 + 32)
        kall[3, core, quarter, :, :LATENT] = latent[rows, :]
        kall[3, core, quarter, :, LATENT:] = rope[rows, :]
    pl.semaphore_wait(barrier, len(peers))

    own = remote(kall.at[3, core], kall.at[3, core], own_s, own_r, sibling)
    ahead = [
        remote(
            kall.at[3, core, y],
            kall.at[3 - step, core, y],
            ctx_s.at[step - 1],
            ctx_r.at[step - 1],
            chip_at(step),
        )
        for step in (1, 2, 3)
    ]
    for copy in ahead:
        copy.start()
    own.start()

    row, col = iota((NOPE, NOPE), 0), iota((NOPE, NOPE), 1)
    owner = ((row >> 4) & 3) * 32 + ((row >> 2) & 3) * 8 + (row >> 6) * 4 + (row & 3)
    by_owner = (col == owner).astype(F32).astype(BF16)
    eye = (col == row).astype(F32).astype(BF16)
    row, col = iota((64, 64), 0), iota((64, 64), 1)
    by_z = (col == ((row >> 2) & 3) * 16 + (row >> 4) * 4 + (row & 3)).astype(F32).astype(BF16)

    lane = iota((TOK, 2 * ROPE), 1)

    def project(head, carry):
        rows = pl.ds(pl.multiple_of(head * TOK, TOK), TOK)
        cols = pl.ds(pl.multiple_of(lax.div(head, 2) * 2 * ROPE, 2 * ROPE), 2 * ROPE)
        mine = gq_t[head]
        q_all[rows, :LATENT] = nn(mine, wk[head]).astype(BF16)
        keep = (lane < ROPE) == (lax.rem(head, 2) == 0)
        q_all[rows, LATENT:] = jnp.where(keep, q_rope[:, cols], jnp.zeros((), BF16))
        qt[head] = nt(by_owner, mine).astype(BF16)
        gt_all[:, rows] = nt(wv[head], og[head]).astype(BF16)
        return carry

    for copy in loads:
        copy.wait()
    gq_t[...] = jnp.swapaxes(q_in[...], 0, 1)
    og[...] = jnp.swapaxes(og_in[...], 0, 1)
    lax.fori_loop(0, HEADS // 2, project, 0)

    around = []
    for near in (1, 2, 3):
        ahead[near - 1].wait_recv()
        part = kall.at[3 - near, core, y]
        around.append(
            [
                remote(
                    part,
                    part,
                    yag_s.at[near - 1, step - 1],
                    yag_r.at[near - 1, step - 1],
                    place(y_=up(y, step)),
                )
                for step in (2, 1, 3)
            ]
        )
        for copy in around[-1]:
            copy.start()

    lax.fori_loop(HEADS // 2, HEADS, project, 0)

    query_pos = me * TOK + iota((1, TOK), 1)
    doc_start = jnp.zeros((1, TOK), jnp.int32)
    begin = jnp.int32(0)
    for doc in range(lengths.shape[0]):
        end = begin + lengths[doc]
        inside = (query_pos >= begin) & (query_pos < end)
        doc_start = doc_start + jnp.where(inside, begin, 0)
        begin = end
    for block in range(SPAN + 1):
        key_pos = (me - SPAN + block) * TOK + iota((TOK, TOK), 0)
        allowed = (key_pos >= doc_start) & (key_pos <= query_pos)
        bias[block * TOK : (block + 1) * TOK, :] = jnp.where(allowed, 0.0, -jnp.inf).astype(F32)

    def place_keys(block):
        at = core + block
        keys = kall[lax.div(at, 2), lax.rem(at, 2)].reshape(TOK, WIDE)
        kw[block * TOK : (block + 1) * TOK, :] = keys
        kwt[:, block * TOK : (block + 1) * TOK] = keys.T

    place_keys(6)
    across = []
    for near in (1, 2, 3):
        for copy in around[near - 1]:
            copy.wait_recv()
        part = kall.at[3 - near, core]
        across.append(remote(part, part, sib_s.at[near - 1], sib_r.at[near - 1], sibling))
        across[-1].start()
    own.wait_recv()
    for near in (1, 2, 3):
        across[near - 1].wait_recv()
        place_keys(7 - 2 * near)
        place_keys(6 - 2 * near)

    def w_stage0(g):
        return remote(w_out.at[g, other], w_r0.at[g], w0_s.at[g], w0_r.at[g], sibling)

    def w_stage1(g):
        return [
            remote(
                w_out.at[g, core, up(x, step)],
                w_r1.at[g, step - 1],
                w1_s.at[g, step - 1],
                w1_r.at[g, step - 1],
                place(x_=up(x, step)),
            )
            for step in (2, 1, 3)
        ]

    def w_stage2(g):
        return [
            remote(
                w_v.at[g, up(z, step)],
                w_rz.at[g, step - 1],
                wz_s.at[g, step - 1],
                wz_r.at[g, step - 1],
                place(z_=up(z, step)),
            )
            for step in (1, 2, 3)
        ]

    def w_do1(g):
        w_stage0(g).wait_recv()

        def one(part, carry):
            w_out[g, core, part] = add(w_out[g, core, part], w_r0[g, part]).astype(BF16)
            return carry

        lax.fori_loop(0, 4, one, 0)
        for copy in w_stage1(g):
            copy.start()

    def w_do2(g, of_key):
        for copy in w_stage1(g):
            copy.wait_recv()
        total = add(w_out[g, core, x], w_r1[g, 0], w_r1[g, 1], w_r1[g, 2]).astype(BF16)
        if of_key:
            total = nn(by_z, total).astype(BF16)
            for part in range(4):
                w_v[g, part] = total[part * 16 : part * 16 + 16, :]
        else:
            for part in range(4):
                for head in range(PACK):
                    w_v[g, part, :, head * 128 : head * 128 + 128] = total[
                        head * 16 : head * 16 + 16, part * 128 : part * 128 + 128
                    ]
        for copy in w_stage2(g):
            copy.start()

    def w_do3(g, of_key):
        for copy in w_stage2(g):
            copy.wait_recv()
        total = add(w_v[g, z], w_rz[g, 0], w_rz[g, 1], w_rz[g, 2]).astype(BF16)
        for local in range(PACK):
            if of_key:
                g_wk[(g - GROUPS) * PACK + local] = total[local * 4 : local * 4 + 4, :]
            else:
                g_wv[g * PACK + local] = total[:, local * 128 : local * 128 + 128]

    def group(g, carry):
        cols = pl.ds(pl.multiple_of(g * COLS, COLS), COLS)
        s_buf[...] = nt(kw[...], q_all[cols, :])
        high = jnp.full((1, COLS), -jnp.inf, F32)
        for block in range(SPAN + 1):
            rows = slice(block * TOK, (block + 1) * TOK)
            part = s_buf[rows, :] * SCALE + jnp.concatenate([bias[rows, :]] * PACK, axis=1)
            s_buf[rows, :] = part
            high = jnp.maximum(high, jnp.max(part, axis=0, keepdims=True))
        total = jnp.zeros((1, COLS), F32)
        for block in range(SPAN + 1):
            rows = slice(block * TOK, (block + 1) * TOK)
            part = jnp.exp(s_buf[rows, :] - high)
            s_buf[rows, :] = part
            total = total + jnp.sum(part, axis=0, keepdims=True)
        share = 1.0 / total
        for block in range(SPAN + 1):
            rows = slice(block * TOK, (block + 1) * TOK)
            part = s_buf[rows, :] * share
            s_buf[rows, :] = part
            p_all[rows, cols] = part.astype(BF16)

        @pl.when(g > 0)
        def _():
            w_do1(g - 1)

        gp_buf[...] = nn(kw[:, :LATENT], gt_all[:, cols])
        out_t = nn(kwt[:LATENT, :], p_all[:, cols]).astype(BF16)
        correction = jnp.sum(out_t.astype(F32) * gt_all[:, cols].astype(F32), axis=0, keepdims=True)
        for block in range(SPAN + 1):
            rows = slice(block * TOK, (block + 1) * TOK)
            part = SCALE * s_buf[rows, :] * (gp_buf[rows, :] - correction)
            ds_all[rows, cols] = part.astype(BF16)

        for local in range(PACK):
            gwv = nn(out_t[:, local * TOK : (local + 1) * TOK], og[g * PACK + local]).astype(BF16)
            rows = slice(local * 16, local * 16 + 16)
            for half in range(2):
                for part in range(4):
                    for depth in range(4):
                        begin = ((part * 4 + depth) * 2 + half) * 16
                        w_out[g, half, part, rows, depth * 128 : depth * 128 + 128] = gwv[
                            begin : begin + 16, :
                        ]
        w_stage0(g).start()

        @pl.when(g > 1)
        def _():
            w_do2(g - 2, False)

        return carry

    def query_terms(g):
        cols = slice(g * COLS, (g + 1) * COLS)
        dq_all[g] = nn(kwt[...], ds_all[:, cols]).astype(BF16)
        for local in range(PACK):
            mine = dq_all[g, :LATENT, local * TOK : (local + 1) * TOK]
            gwk = nt(qt[g * PACK + local], mine).astype(BF16)
            rows = slice(local * 16, local * 16 + 16)
            for half in range(2):
                for part in range(4):
                    begin = half * 64 + part * 16
                    w_out[GROUPS + g, half, part, rows, :] = gwk[begin : begin + 16, :]
        w_stage0(GROUPS + g).start()

    def query_out(g):
        for local in range(PACK):
            head = g * PACK + local
            mine = dq_all[g, :LATENT, local * TOK : (local + 1) * TOK]
            gq_t[head] = nt(eye, nn(wk[head], mine).astype(BF16)).astype(BF16)
        for pair in range(PACK // 2):
            left = dq_all[g, LATENT : LATENT + ROPE, pair * 256 : pair * 256 + 128]
            right = dq_all[g, LATENT + ROPE :, pair * 256 + 128 : pair * 256 + 256]
            both = nt(eye, jnp.concatenate([left, right], axis=0)).astype(BF16)
            gqr_v[:, (g * 2 + pair) * 128 : (g * 2 + pair + 1) * 128] = both

    lax.fori_loop(0, GROUPS, group, 0)
    last = GROUPS - 1

    def key_terms(first, after, between):
        rows = slice(first * TOK, after * TOK)
        wide = nn(ds_all[rows, :], q_all[...])
        between()
        narrow = wide[:, :LATENT] + nt(p_all[rows, :], gt_all[...])
        narrow, side = narrow.astype(BF16), wide[:, LATENT:].astype(BF16)
        for block in range(first, after):
            for quarter in range(4):
                for half in range(2):
                    begin = (block - first) * TOK + quarter * 32 + half * 16
                    kg[half, quarter, core + block, :, :LATENT] = narrow[begin : begin + 16, :]
                    kg[half, quarter, core + block, :, LATENT:] = side[begin : begin + 16, :]

    def e0(n):
        blocks = pl.ds(4 * n, 4)
        return remote(
            kg.at[other, :, blocks], k_r0.at[:, blocks], e0_s.at[n], e0_r.at[n], sibling
        )

    def e1(n):
        blocks = pl.ds(4 * n, 4)
        return [
            remote(
                kg.at[core, up(y, step), blocks],
                k_r1.at[n, step - 1],
                e1_s.at[n, step - 1],
                e1_r.at[n, step - 1],
                place(y_=up(y, step)),
            )
            for step in (2, 1, 3)
        ]

    def e3(step):
        return remote(
            k_sum.at[pl.ds((3 - step) * 2, 2)],
            k_r3.at[step - 1],
            e3_s.at[step - 1],
            e3_r.at[step - 1],
            chip_at(-step),
        )

    def k_do1(n):
        e0(n).wait_recv()
        blocks = slice(4 * n, 4 * n + 4)
        for quarter in range(4):
            kg[core, quarter, blocks] = add(kg[core, quarter, blocks], k_r0[quarter, blocks]).astype(
                BF16
            )
        for copy in e1(n):
            copy.start()

    def k_do2(n):
        for copy in e1(n):
            copy.wait_recv()
        blocks = slice(4 * n, 4 * n + 4)
        k_sum[blocks] = add(kg[core, y, blocks], k_r1[n, 0], k_r1[n, 1], k_r1[n, 2]).astype(BF16)
        for step in ((3, 2), (1,))[n]:
            e3(step).start()

    for half in range(2):
        for quarter in range(4):
            kg[half, quarter, 7 * other] = jnp.zeros((16, WIDE), BF16)
    key_terms(0, 4, lambda: w_do1(last))
    e0(0).start()
    key_terms(4, 7, lambda: k_do1(0))
    e0(1).start()
    w_do2(last - 1, False)
    query_terms(0)
    k_do1(1)
    query_terms(1)
    w_do1(GROUPS)
    w_do2(last, False)
    query_terms(2)
    w_do1(GROUPS + 1)
    query_terms(3)
    w_do1(GROUPS + 2)
    query_out(0)
    k_do2(0)
    w_do1(GROUPS + 3)
    query_out(1)
    query_out(2)
    k_do2(1)
    w_do2(GROUPS, True)
    query_out(3)
    gq_v[...] = jnp.swapaxes(gq_t[...], 0, 1)
    leave = [
        pltpu.make_async_copy(gq_v, gq, leave_s.at[0]),
        pltpu.make_async_copy(gqr_v, gq_rope, leave_s.at[1]),
    ]
    for copy in leave:
        copy.start()
    w_do2(GROUPS + 1, True)
    for step in (1, 2, 3):
        e3(step).wait_recv()
    k_mid[...] = add(k_sum[6:8], k_r3[0], k_r3[1], k_r3[2]).astype(BF16)
    e4 = remote(k_mid, k_r4, e4_s, e4_r, place(zh_=1 - zh))
    e4.start()
    w_do2(GROUPS + 2, True)
    for g in range(GROUPS):
        w_do3(g, False)
    e4.wait_recv()
    total = add(k_mid[...], k_r4[...])
    k_fin[:, :, :LATENT] = total[:, :, :LATENT].astype(BF16)
    rope_part = total[:, :, LATENT:].reshape(32, 2 * ROPE)
    rope_part = rope_part + pltpu.roll(rope_part, ROPE, 1)
    k_fin[:, :, LATENT:] = rope_part.reshape(2, 16, 2 * ROPE).astype(BF16)
    k_out[y, core] = k_fin[core]
    e5 = [
        remote(
            k_fin.at[core],
            k_out.at[y, core],
            e5_s.at[step - 1],
            e5_r.at[step - 1],
            place(y_=up(y, step)),
        )
        for step in (1, 2, 3)
    ] + [
        remote(
            k_fin.at[other],
            k_out.at[y, core],
            e5_s.at[3 + step],
            e5_r.at[3 + step],
            place(y_=up(y, step), core_=other),
        )
        for step in (0, 1, 2, 3)
    ]
    for copy in e5:
        copy.start()
    w_do2(GROUPS + 3, True)
    w_do3(GROUPS, True)
    w_do3(GROUPS + 1, True)
    for copy in e5:
        copy.wait_recv()
    for quarter in range(4):
        for half in range(2):
            begin = quarter * 32 + half * 16
            g_latent[begin : begin + 16, :] = k_out[quarter, half, :, :LATENT]
    g_rope_t[...] = k_out[:, :, :, LATENT:].reshape(TOK, 2 * ROPE).T[:ROPE, :]
    w_do3(GROUPS + 2, True)
    w_do3(GROUPS + 3, True)
    for copy in leave:
        copy.wait()

    own.wait_send()
    e4.wait_send()
    for n in range(2):
        for copy in [e0(n), *e1(n)]:
            copy.wait_send()
    for copy in [*ahead, *across, *e5, *(copy for three in around for copy in three)]:
        copy.wait_send()
    for step in (1, 2, 3):
        e3(step).wait_send()
    for g in range(JOBS):
        for copy in [w_stage0(g), *w_stage1(g), *w_stage2(g)]:
            copy.wait_send()


def hand_over(*refs):
    count = len(refs) // 2
    for source, target in zip(refs[:count], refs[count:]):
        target[...] = source[...]


def per_device(q_nope, q_rope, latent, k_rope, out_grad, w_key, w_value, lengths):
    dma = pltpu.SemaphoreType.DMA
    vmem = pl.BlockSpec(memory_space=pltpu.VMEM)
    hbm = pl.BlockSpec(memory_space=pl.ANY)

    def held(*shape, dtype=BF16):
        return pltpu.VMEM(shape, dtype)

    out = pl.pallas_call(
        kernel,
        out_shape=(
            jax.ShapeDtypeStruct((TOK, HEADS, NOPE), BF16),
            jax.ShapeDtypeStruct((TOK, HEADS * ROPE), BF16),
            jax.ShapeDtypeStruct((TOK, LATENT), BF16),
            jax.ShapeDtypeStruct((ROPE, TOK), BF16),
            jax.ShapeDtypeStruct((HEADS, 4, LATENT), BF16),
            jax.ShapeDtypeStruct((HEADS, 16, NOPE), BF16),
        ),
        in_specs=[pl.BlockSpec(memory_space=pltpu.SMEM), hbm, hbm, vmem, vmem, hbm, hbm, hbm],
        out_specs=[hbm] * 2 + [vmem] * 4,
        scratch_shapes=[
            held(TOK, HEADS, NOPE),
            held(TOK, HEADS, NOPE),
            held(TOK, HEADS * ROPE),
            held(HEADS, NOPE, LATENT),
            held(HEADS, LATENT, NOPE),
            held(HEADS, TOK, NOPE),
            held(HEADS, NOPE, TOK),
            held(HEADS, TOK, NOPE),
            held(TOK, HEADS, NOPE),
            held(TOK, HEADS * ROPE),
            held(GROUPS, WIDE, COLS),
            held(4, 2, 4, 32, WIDE),
            held(WINDOW, WIDE),
            held(WIDE, WINDOW),
            held(HEADS * TOK, WIDE),
            held(LATENT, HEADS * TOK),
            held(WINDOW, HEADS * TOK),
            held(WINDOW, HEADS * TOK),
            held(WINDOW, COLS, dtype=F32),
            held(WINDOW, COLS, dtype=F32),
            held(WINDOW, TOK, dtype=F32),
            held(JOBS, 2, 4, 64, LATENT),
            held(JOBS, 4, 64, LATENT),
            held(JOBS, 3, 64, LATENT),
            held(JOBS, 4, 16, LATENT),
            held(JOBS, 3, 16, LATENT),
            held(2, 4, 8, 16, WIDE),
            held(4, 8, 16, WIDE),
            held(2, 3, 4, 16, WIDE),
            held(8, 16, WIDE),
            held(3, 2, 16, WIDE),
            held(2, 16, WIDE),
            held(2, 16, WIDE),
            held(2, 16, WIDE),
            held(4, 2, 16, WIDE),
            dma((5,)),
            dma((2,)),
            dma,
            dma,
            dma((3,)),
            dma((3,)),
            dma((3, 3)),
            dma((3, 3)),
            dma((3,)),
            dma((3,)),
            dma((JOBS,)),
            dma((JOBS,)),
            dma((JOBS, 3)),
            dma((JOBS, 3)),
            dma((JOBS, 3)),
            dma((JOBS, 3)),
            dma((2,)),
            dma((2,)),
            dma((2, 3)),
            dma((2, 3)),
            dma((3,)),
            dma((3,)),
            dma,
            dma,
            dma((7,)),
            dma((7,)),
        ],
        compiler_params=pltpu.CompilerParams(
            collective_id=0, has_side_effects=True, vmem_limit_bytes=58 * 2**20
        ),
        cost_estimate=pl.CostEstimate(
            flops=15 * 10**9, bytes_accessed=8 * 10**6, transcendentals=2 * 10**6
        ),
        name="mla_backward",
    )(
        lengths,
        q_nope,
        q_rope,
        latent,
        k_rope.T,
        out_grad,
        w_key,
        w_value,
    )
    gq, gq_rope, g_latent, g_rope_t, g_wk, g_wv = pl.pallas_call(
        hand_over,
        out_shape=tuple(jax.ShapeDtypeStruct(array.shape, array.dtype) for array in out),
        in_specs=[vmem] * len(out),
        out_specs=[vmem] * len(out),
        name="hand_over",
    )(*out)
    return gq, gq_rope, g_latent, g_rope_t.T, g_wk, g_wv


def solution(mesh):
    placed = (
        P("ctx", "tp", None),
        P("ctx", "tp"),
        P("ctx", None),
        P("ctx", None),
        P("ctx", "tp", None),
        P("tp", None, None),
        P("tp", None, None),
        P(),
    )
    return jax.shard_map(
        per_device,
        mesh=mesh,
        in_specs=placed,
        out_specs=(
            P("ctx", "tp", None),
            P("ctx", "tp"),
            P("ctx", None),
            P("ctx", None),
            P("tp", "ctx", None),
            P("tp", "ctx", None),
        ),
        check_vma=False,
    )
```
